32 devices in a mesh: seq: 8 (over z, y), head: 4 (over x, core).
Axes of the slice: x: 2, y: 2, z: 4, core: 2. Of those that a mesh axis runs over, the one named last changes fastest.
Arguments:
- ssd_input: bfloat16 [4096, 128, 128], P('seq', 'head'), may hold values from -3 to 3
- log_decay: float32 [4096, 128], P('seq', 'head'), may hold values from -1.6 to 0, as said below
- input_map: float32 [4096, 8, 128], P('seq', 'head'), may hold values from -0.18 to 0.18
- output_map: float32 [4096, 8, 128], P('seq', 'head'), may hold values from -0.18 to 0.18
- ssd_cotangent: bfloat16 [4096, 128, 128], P('seq', 'head'), may hold values from -3 to 3
- queries: bfloat16 [4096, 8, 128], P('seq', 'head'), may hold values from -100 to 100
- key_rows: bfloat16 [4096, 128], P('seq'), may hold values from -4 to 4
- value_rows: bfloat16 [4096, 128], P('seq'), may hold values from -6 to 6
- attn_cotangent: bfloat16 [4096, 8, 128], P('seq', 'head'), may hold values from -6 to 6
- pair_order: int32 [8], replicated, may hold values from 0 to 7, each once
Outputs:
- grad_input: bfloat16 [4096, 128, 128], P('seq', 'head')
- grad_decay: float32 [4096, 128], P('seq', 'head')
- grad_input_map: float32 [4096, 8, 128], P('seq', 'head')
- grad_output_map: float32 [4096, 8, 128], P('seq', 'head')
- grad_queries: bfloat16 [4096, 8, 128], P('seq', 'head')
- grad_keys: bfloat16 [4096, 128], P('seq')
- grad_values: bfloat16 [4096, 128], P('seq')
The draws below stay inside these ranges and needn't reach their ends.
Inputs may be any that keep to these rules, and one draw needn't show every extreme that they name: `pair_order`: a permutation of 0 to 7. `log_decay`: negative everywhere.
All inputs are finite; a program needn't handle non-finite values.
Results may differ from the reference program's by a relative error of at most 0.035.
Values may be sent and summed in bfloat16 or wider, within the bound.
A program may use at most 192 MiB of HBM per device.

```python
import math
import jax
import jax.numpy as jnp
from jax import lax

SCAN_HEADS = 128
GROUPS = 8
HEAD_DIM = 128
STATE = 128
Q_HEADS = 8
ATT_DIM = 128
BLOCK = 128
TOK_DEV = 512
SEQUENCE_TOKENS = 4096
HALF = 256
N_SEQ = 8


def draw_log_decay(key, part):
    segments = jax.random.split(key, 7)
    fast_share = 0.5
    fast_heads = jax.random.uniform(segments[0], (SCAN_HEADS,)) < fast_share
    fast_rate = jnp.exp(jax.random.uniform(segments[1], (SCAN_HEADS,), minval=math.log(1.0 / 50.0), maxval=math.log(1.0 / 30.0)))
    slow_rate = jnp.exp(jax.random.uniform(segments[2], (SCAN_HEADS,), minval=math.log(0.1), maxval=math.log(0.4))) / SEQUENCE_TOKENS
    baseline_rate = jnp.where(fast_heads, fast_rate, slow_rate)
    block_multiplier = jnp.exp(jax.random.uniform(segments[3], (SEQUENCE_TOKENS // TOK_DEV, SCAN_HEADS), minval=math.log(0.5), maxval=math.log(2.0)))
    block_multiplier = jnp.repeat(block_multiplier, TOK_DEV, axis=0)
    token_multiplier = jax.random.uniform(segments[4], (SEQUENCE_TOKENS, SCAN_HEADS), minval=0.5, maxval=1.5)
    packet_rows = jax.random.randint(segments[5], (2,), 0, SEQUENCE_TOKENS)
    packet_size = jax.random.uniform(segments[6], (2, SCAN_HEADS), minval=0.22, maxval=0.69)
    row_position = jnp.arange(SEQUENCE_TOKENS)
    packets = jnp.where(row_position[:, None] == packet_rows[0], packet_size[0][None, :], 0.0)
    packets = packets + jnp.where(row_position[:, None] == packet_rows[1], packet_size[1][None, :], 0.0)
    return (-(baseline_rate[None, :] * block_multiplier * token_multiplier + packets)).astype(jnp.float32)


def attention_pair(key):
    base_key = jax.random.fold_in(key, 11)
    segments = jax.random.split(base_key, 2)
    key_draw = jnp.clip(jax.random.normal(segments[0], (SEQUENCE_TOKENS, ATT_DIM)), -4.0, 4.0)
    query_draw = jnp.clip(jax.random.normal(segments[1], (SEQUENCE_TOKENS, Q_HEADS, ATT_DIM)), -6.0, 6.0)
    return (query_draw, key_draw)


def draw_queries(key, part):
    return attention_pair(key)[0].astype(jnp.bfloat16)


def draw_key_rows(key, part):
    return attention_pair(key)[1].astype(jnp.bfloat16)


def steps_of(rng, dims, cuts, least, top_value):
    def one(axis_at, parts):
        heights = jax.random.uniform(jax.random.fold_in(jax.random.fold_in(rng, 6), axis_at), (parts,), jnp.float32, least / len(cuts), top_value / len(cuts))
        return jnp.repeat(jnp.exp(heights), dims[axis_at] // parts).reshape((-1,) + (1,) * (len(dims) - axis_at - 1))

    factor_of = one(*cuts[0])
    for cut in cuts[1:]:
        factor_of = factor_of * one(*cut)
    return factor_of


def normal_values(stream_key, extent, width, most, shards=(), held_as=jnp.bfloat16):
    array = jax.random.normal(stream_key, extent, jnp.float32) * width
    if len(shards) > 0:
        array = steps_of(stream_key, extent, shards, -0.22, 0.18) * array
    return jnp.clip(array, min=-most, max=most).astype(held_as)


def setup_inputs(seed: int = 0) -> dict:
    seeds = jax.random.split(jax.random.key(seed), 11)
    return {
        "ssd_input": normal_values(seeds[0], (SEQUENCE_TOKENS, SCAN_HEADS, HEAD_DIM), 0.5, 3.0, ((0, 8), (1, 4))),
        "log_decay": draw_log_decay(jax.random.fold_in(seeds[10], 71), 0),
        "input_map": normal_values(seeds[2], (SEQUENCE_TOKENS, GROUPS, STATE), 0.03, 0.18, ((0, 8), (1, 4)), jnp.float32),
        "output_map": normal_values(seeds[3], (SEQUENCE_TOKENS, GROUPS, STATE), 0.03, 0.18, ((0, 8), (1, 4)), jnp.float32),
        "ssd_cotangent": normal_values(seeds[4], (SEQUENCE_TOKENS, SCAN_HEADS, HEAD_DIM), 0.5, 3.0, ((0, 8), (1, 4))),
        "queries": draw_queries(jax.random.fold_in(seeds[10], 71), 0),
        "key_rows": draw_key_rows(jax.random.fold_in(seeds[10], 71), 0),
        "value_rows": normal_values(seeds[7], (SEQUENCE_TOKENS, ATT_DIM), 1.0, 6.0, ((0, 8),)),
        "attn_cotangent": normal_values(seeds[8], (SEQUENCE_TOKENS, Q_HEADS, ATT_DIM), 1.0, 6.0, ((0, 8), (1, 4))),
        "pair_order": jax.random.permutation(seeds[9], N_SEQ).astype(jnp.int32),
    }


HIGHEST = lax.Precision.HIGHEST
NEG_FILL = -1e+30

def through_bf16(values):
    return lax.optimization_barrier(values.astype(jnp.bfloat16)).astype(jnp.float32)

def block_advance(state_now, inputs):
    x_block, a_block, b_block, c_block = inputs
    cumulative = jnp.cumsum(a_block, axis=0)
    block_len = a_block.shape[0]
    causal_mask = (jnp.arange(block_len)[:, None] >= jnp.arange(block_len)[None, :])[:, :, None, None]
    decay_grid = jnp.exp(jnp.where(causal_mask, cumulative[:, None] - cumulative[None, :], NEG_FILL))
    inner_prod = jnp.einsum('tgn,sgn->tsg', c_block, b_block, precision=HIGHEST)
    weight_grid = through_bf16(inner_prod[:, :, :, None] * decay_grid)
    x_wide = x_block.astype(jnp.float32)
    local_part = jnp.einsum('tsge,sgep->tgep', weight_grid, x_wide, precision=HIGHEST)
    c_scaled = through_bf16(c_block[:, :, None, :] * jnp.exp(cumulative)[..., None])
    carried_part = jnp.einsum('tgen,genp->tgep', c_scaled, through_bf16(state_now), precision=HIGHEST)
    block_out = (local_part + carried_part).astype(jnp.bfloat16)
    tail_decay = jnp.exp(cumulative[-1][None] - cumulative)
    b_scaled = through_bf16(b_block[:, :, None, :] * tail_decay[..., None])
    fresh_state = jnp.einsum('tgen,tgep->genp', b_scaled, x_wide, precision=HIGHEST)
    return (jnp.exp(cumulative[-1])[..., None, None] * state_now + fresh_state, block_out)

def blocked(values):
    return values.reshape((values.shape[0] // BLOCK, BLOCK) + values.shape[1:])

def run_blocks(x_seq, a_seq, b_seq, c_seq, state_start):
    state_end, block_outs = lax.scan(block_advance, state_start, (blocked(x_seq), blocked(a_seq), blocked(b_seq), blocked(c_seq)))
    return (block_outs.reshape(x_seq.shape), state_end)

def group_backward(group_items):
    x_group, a_group, b_group, c_group, dy_group = group_items
    per_group = x_group.shape[1]

    def forward(x_values, a_values, b_values, c_values):
        state_zero = jnp.zeros((1, per_group, STATE, HEAD_DIM), jnp.float32)
        result, ignored = run_blocks(x_values[:, None], a_values[:, None], b_values[:, None], c_values[:, None], state_zero)
        return result[:, 0]
    primal, pullback = jax.vjp(forward, x_group, a_group, b_group, c_group)
    return pullback(dy_group)

def attention_grads(queries, key_rows, value_rows, attn_cotangent, pair_order):
    row_position = jnp.arange(SEQUENCE_TOKENS, dtype=jnp.int32)
    owner_dev = row_position // TOK_DEV
    within = row_position % TOK_DEV
    first_block = pair_order[owner_dev]
    block_id = jnp.where(within < HALF, first_block, 2 * N_SEQ - 1 - first_block)
    position = block_id * HALF + within % HALF
    keys_wide = key_rows.astype(jnp.float32)
    values_wide = value_rows.astype(jnp.float32)
    scale_factor = ATT_DIM ** (-0.5)

    def query_block(carried, block_index):
        key_grad, value_grad = carried
        start_row = (block_index * HALF).astype(jnp.int32)
        query_part = lax.dynamic_slice_in_dim(queries, start_row, HALF, 0).astype(jnp.float32)
        grad_part = lax.dynamic_slice_in_dim(attn_cotangent, start_row, HALF, 0).astype(jnp.float32)
        query_at = lax.dynamic_slice_in_dim(position, start_row, HALF, 0)
        visible = position[None, :] <= query_at[:, None]
        scores = jnp.einsum('rhd,kd->hrk', query_part, keys_wide, precision=HIGHEST) * scale_factor
        scores = jnp.where(visible[None], scores, NEG_FILL)
        row_top = lax.optimization_barrier(jnp.max(scores, axis=-1, keepdims=True))
        exp_scores = jnp.exp(scores - row_top)
        probs = exp_scores / lax.optimization_barrier(jnp.sum(exp_scores, axis=-1, keepdims=True))
        prob_b = through_bf16(probs)
        attn_out = through_bf16(jnp.einsum('hrk,kd->rhd', prob_b, values_wide, precision=HIGHEST))
        row_delta = lax.optimization_barrier(jnp.sum(grad_part * attn_out, axis=-1))
        prob_grad = jnp.einsum('rhd,kd->hrk', grad_part, values_wide, precision=HIGHEST)
        dscore = through_bf16(probs * (prob_grad - row_delta.T[:, :, None]))
        query_grad = (jnp.einsum('hrk,kd->rhd', dscore, keys_wide, precision=HIGHEST) * scale_factor).astype(jnp.bfloat16)
        key_grad = key_grad + jnp.einsum('hrk,rhd->kd', dscore, query_part, precision=HIGHEST) * scale_factor
        value_grad = value_grad + jnp.einsum('hrk,rhd->kd', prob_b, grad_part, precision=HIGHEST)
        return ((key_grad, value_grad), query_grad)
    zero_grad = jnp.zeros((SEQUENCE_TOKENS, ATT_DIM), jnp.float32)
    sums, query_blocks = lax.scan(query_block, (zero_grad, zero_grad), jnp.arange(SEQUENCE_TOKENS // HALF, dtype=jnp.int32))
    grad_queries = query_blocks.reshape(SEQUENCE_TOKENS, Q_HEADS, ATT_DIM)
    return (grad_queries, sums[0].astype(jnp.bfloat16), sums[1].astype(jnp.bfloat16))

def reference(ssd_input, log_decay, input_map, output_map, ssd_cotangent, queries, key_rows, value_rows, attn_cotangent, pair_order):
    per_group = SCAN_HEADS // GROUPS
    x_groups = ssd_input.reshape(SEQUENCE_TOKENS, GROUPS, per_group, HEAD_DIM).transpose(1, 0, 2, 3)
    a_groups = log_decay.reshape(SEQUENCE_TOKENS, GROUPS, per_group).transpose(1, 0, 2)
    b_groups = input_map.transpose(1, 0, 2)
    c_groups = output_map.transpose(1, 0, 2)
    dy_groups = ssd_cotangent.reshape(SEQUENCE_TOKENS, GROUPS, per_group, HEAD_DIM).transpose(1, 0, 2, 3)
    gradients = lax.map(group_backward, (x_groups, a_groups, b_groups, c_groups, dy_groups))
    grad_input = gradients[0].transpose(1, 0, 2, 3).reshape(SEQUENCE_TOKENS, SCAN_HEADS, HEAD_DIM)
    grad_decay = gradients[1].transpose(1, 0, 2).reshape(SEQUENCE_TOKENS, SCAN_HEADS)
    grad_input_map = gradients[2].transpose(1, 0, 2)
    grad_output_map = gradients[3].transpose(1, 0, 2)
    grad_queries, grad_keys, grad_values = attention_grads(queries, key_rows, value_rows, attn_cotangent, pair_order)
    return (grad_input, grad_decay, grad_input_map, grad_output_map, grad_queries, grad_keys, grad_values)
```

```python
import functools
import math

import jax
import jax.numpy as jnp
from jax import lax
from jax.experimental import pallas as pl
from jax.experimental.pallas import tpu as pltpu
from jax.sharding import PartitionSpec as P

BLOCK = 128
HIGHEST = lax.Precision.HIGHEST
NEG_FILL = -1e30
F32 = jnp.float32
BF16 = jnp.bfloat16
VMEM_BYTES = 52 * 1024 * 1024


def dot(a, b):
    return jnp.dot(a, b, preferred_element_type=F32)


def dot_t(a, b):
    return lax.dot_general(a, b, (((1,), (1,)), ((), ())), preferred_element_type=F32)


def dot_hi(a, b):
    return jnp.dot(a, b, preferred_element_type=F32, precision=HIGHEST)


def iota2(shape, dim):
    return lax.broadcasted_iota(jnp.int32, shape, dim)


def lower_ones():
    shape = (BLOCK, BLOCK)
    return (iota2(shape, 0) >= iota2(shape, 1)).astype(F32)


def upper_ones():
    shape = (BLOCK, BLOCK)
    return (iota2(shape, 0) <= iota2(shape, 1)).astype(F32)


def state_kernel(x_ref, dy_ref, a_ref, b_ref, c_ref, s_ref, p_ref, tot_ref, tx, ey):
    rows, heads = a_ref.shape[1:]
    width = x_ref.shape[1] // heads
    lower = lower_ones()
    offset = jnp.zeros((1, heads), F32)
    cums = []
    for k in range(rows // BLOCK):
        cum = dot_hi(lower, a_ref[0, pl.ds(k * BLOCK, BLOCK), :])
        cums.append(cum + offset)
        offset = offset + cum[BLOCK - 1 :, :]
    tot_ref[0] = offset
    for k, cum in enumerate(cums):
        span = pl.ds(k * BLOCK, BLOCK)
        tail = jnp.exp(offset - cum)
        head_decay = jnp.exp(cum)
        for h in range(heads):
            lanes = pl.ds(h * width, width)
            tx[span, lanes] = (x_ref[span, lanes].astype(F32) * tail[:, h : h + 1]).astype(BF16)
            ey[span, lanes] = (
                dy_ref[span, lanes].astype(F32) * head_decay[:, h : h + 1]
            ).astype(BF16)
    b_t = b_ref[...].T.astype(BF16)
    c_t = c_ref[...].T.astype(BF16)
    step = 4 * width
    for at in range(0, heads * width, step):
        lanes = pl.ds(at, step)
        s_ref[0, :, lanes] = dot(b_t, tx[:, lanes]).astype(BF16)
        p_ref[0, :, lanes] = dot(c_t, ey[:, lanes]).astype(BF16)


def scan_kernel(
    x_ref,
    dy_ref,
    a_ref,
    at_ref,
    b_ref,
    c_ref,
    s_in,
    ds_in,
    dx_ref,
    da_ref,
    db_ref,
    dc_ref,
    states,
    tails,
    edy,
    s_now,
    ds_now,
    dgt,
):
    rows, heads = a_ref.shape[1:]
    width = x_ref.shape[1] // heads
    count = rows // BLOCK
    lower = lower_ones()
    upper = upper_ones()
    s_now[...] = s_in[0]
    ds_now[...] = ds_in[0]

    def forward(k, carry):
        span = pl.ds(pl.multiple_of(k * BLOCK, BLOCK), BLOCK)
        cum = dot_hi(lower, a_ref[0, span, :])
        last = cum[BLOCK - 1 :, :]
        tail = jnp.exp(last - cum)
        whole = jnp.exp(last)
        b_t = b_ref[span, :].T.astype(BF16)
        for h in range(heads):
            lanes = pl.ds(h * width, width)
            tails[span, lanes] = (
                x_ref[span, lanes].astype(F32) * tail[:, h : h + 1]
            ).astype(BF16)
        for h in range(heads):
            lanes = pl.ds(h * width, width)
            now = s_now[:, lanes]
            states[k, :, lanes] = now.astype(BF16)
            s_now[:, lanes] = now * whole[:, h : h + 1] + dot(b_t, tails[span, lanes])
        return carry

    lax.fori_loop(0, count, forward, 0)
    causal = iota2((BLOCK, BLOCK), 0) <= iota2((BLOCK, BLOCK), 1)

    def backward(turn, carry):
        k = count - 1 - turn
        span = pl.ds(pl.multiple_of(k * BLOCK, BLOCK), BLOCK)
        cum = dot_hi(lower, a_ref[0, span, :])
        cum_t = dot_hi(at_ref[0, :, span], upper)
        last = cum[BLOCK - 1 :, :]
        tail = jnp.exp(last - cum)
        whole = jnp.exp(last)
        grow = jnp.exp(cum)
        b_wide = b_ref[span, :]
        c_wide = c_ref[span, :]
        b_low = b_wide.astype(BF16)
        c_low = c_wide.astype(BF16)
        c_t = c_wide.T.astype(BF16)
        gt = lax.dot_general(
            b_wide, c_wide, (((1,), (1,)), ((), ())), preferred_element_type=F32, precision=HIGHEST
        )
        dgt[...] = jnp.zeros_like(dgt)
        columns = jnp.zeros((BLOCK, heads), F32)
        row_sums = jnp.zeros((heads, BLOCK), F32)
        totals = jnp.zeros((heads, BLOCK), F32)
        column_at = iota2((BLOCK, heads), 1)
        row_at = iota2((heads, BLOCK), 0)
        db = jnp.zeros((BLOCK, b_wide.shape[1]), F32)
        dc = jnp.zeros((BLOCK, b_wide.shape[1]), F32)
        for h in range(heads):
            lanes = pl.ds(h * width, width)
            x_h = x_ref[span, lanes]
            dy_h = dy_ref[span, lanes]
            tail_x = tails[span, lanes]
            state = states[k, :, lanes]
            ds_wide = ds_now[:, lanes]
            ds_low = ds_wide.astype(BF16)
            decay = jnp.exp(
                jnp.where(causal, cum_t[h : h + 1, :] - cum[:, h : h + 1], NEG_FILL)
            )
            t1 = dot_t(x_h, dy_h) * decay
            dgt[...] += t1
            mt = t1 * gt
            from_state = dot(b_low, ds_low)
            dx = dot((gt * decay).astype(BF16), dy_h) + from_state * tail[:, h : h + 1]
            dx_ref[span, lanes] = dx.astype(BF16)
            edy_h = (dy_h.astype(F32) * grow[:, h : h + 1]).astype(BF16)
            r2 = tail_x.astype(F32) * from_state
            column = jnp.sum(
                edy_h.astype(F32) * dot(c_low, state) - r2 - mt, axis=1, keepdims=True
            )
            columns = jnp.where(column_at == h, column, columns)
            row_sums = jnp.where(row_at == h, jnp.sum(mt, axis=0, keepdims=True), row_sums)
            total = jnp.sum(r2, axis=0, keepdims=True) + whole[:, h : h + 1] * jnp.sum(
                ds_wide * state.astype(F32), axis=0, keepdims=True
            )
            totals = jnp.where(row_at == h, total, totals)
            dc = dc + dot_t(edy_h, state)
            db = db + dot_t(tail_x, ds_low)
            ds_now[:, lanes] = ds_wide * whole[:, h : h + 1] + dot(c_t, edy_h)
        dg = dgt[...]
        db_ref[span, :] = db + dot_hi(dg, c_wide)
        dc_ref[span, :] = dc + dot_hi(dg.T, b_wide)
        total = jnp.sum(totals, axis=1, keepdims=True)
        row_sums = row_sums + jnp.where(iota2((heads, BLOCK), 1) == BLOCK - 1, total, 0.0)
        da_ref[0, span, :] = dot_hi(upper, columns + row_sums.T)
        return carry

    lax.fori_loop(0, count, backward, 0)


def attention_kernel(
    place_ref, own_ref, q_ref, do_ref, kv_ref, dq_ref, dkv_ref, scores, probs, acc
):
    halves, lanes_q, width = q_ref.shape
    half = kv_ref.shape[0] // place_ref.shape[0]
    scale = width ** (-0.5)
    rate = scale * math.log2(math.e)
    acc[...] = jnp.zeros_like(acc)
    visible = iota2((half, lanes_q), 0) <= lax.rem(iota2((half, lanes_q), 1), half)

    def rows_of(j):
        return pl.ds(pl.multiple_of(place_ref[j] * half, half), half)

    def fold(op, tile):
        return op(tile.reshape(half // 8, 8, lanes_q), axis=0)

    for i in range(halves):
        own = own_ref[i]
        q = q_ref[i]
        q_t = q.T

        def score(j):
            return dot(kv_ref[rows_of(j), :width], q_t)

        def first(j, top):
            tile = score(j)
            scores[j] = tile
            return jnp.maximum(top, fold(jnp.max, tile))

        tile = jnp.where(visible, score(own), NEG_FILL)
        scores[own] = tile
        top = lax.fori_loop(0, own, first, fold(jnp.max, tile))
        top = jnp.max(top, axis=0, keepdims=True) * rate

        def second(j, carry):
            sums, out_t = carry
            prob = jnp.exp2(scores[j] * rate - top)
            low = prob.astype(BF16)
            probs[j] = low
            value_t = kv_ref[rows_of(j), width:].T
            return (sums + fold(jnp.sum, prob), out_t + dot(value_t, low))

        sums, out_t = lax.fori_loop(
            0,
            own + 1,
            second,
            (jnp.zeros((8, lanes_q), F32), jnp.zeros((width, lanes_q), F32)),
        )
        inverse = 1.0 / jnp.sum(sums, axis=0, keepdims=True)
        do_t = do_ref[i].astype(F32).T
        out_low = (out_t * inverse).astype(BF16).astype(F32)
        delta = jnp.sum(do_t * out_low, axis=0, keepdims=True) * inverse
        do_scaled = do_t * inverse
        do_t_low = do_scaled.astype(BF16)
        do_low = do_scaled.T.astype(BF16)

        def third(j, dq_t):
            at = rows_of(j)
            key = kv_ref[at, :width]
            prob = probs[j]
            prob_grad = dot(kv_ref[at, width:], do_t_low)
            ds = (prob.astype(F32) * (prob_grad - delta)).astype(BF16)
            acc[at, :width] += dot(ds, q)
            acc[at, width:] += dot(prob, do_low)
            return dq_t + dot(key.T, ds)

        dq_t = lax.fori_loop(0, own + 1, third, jnp.zeros((width, lanes_q), F32))
        dq_ref[i] = (dq_t * scale).T.astype(BF16)

    quarters, devices, rows = dkv_ref.shape[:3]
    for d in range(devices):
        for u in range(quarters):
            span = pl.ds((d * quarters + u) * rows, rows)
            dkv_ref[u, d, :, :width] = (acc[span, :width] * scale).astype(BF16)
            dkv_ref[u, d, :, width:] = acc[span, width:].astype(BF16)


def spread(weights, width):
    return jnp.repeat(weights, width, axis=-1)[:, None, :]


def states_between(s_own, p_own, tot, width):
    count = lax.axis_size("seq")
    place = lax.axis_index("seq")
    pair = place // 2
    odd = place % 2
    tots = lax.all_gather(tot[:, 0, :], "seq")
    before = jnp.concatenate([jnp.zeros_like(tots[:1]), jnp.cumsum(tots, axis=0)])

    def upto(i):
        return lax.dynamic_index_in_dim(before, jnp.clip(i, 0, count), 0, False)

    swap = [(i, i ^ 1) for i in range(count)]
    other = lax.ppermute(jnp.stack([s_own, p_own]), "seq", swap).astype(F32)
    s_wide, p_wide = s_own.astype(F32), p_own.astype(F32)
    first_s = jnp.where(odd == 1, other[0], s_wide)
    second_s = jnp.where(odd == 1, s_wide, other[0])
    first_p = jnp.where(odd == 1, other[1], p_wide)
    second_p = jnp.where(odd == 1, p_wide, other[1])
    decay_first = spread(jnp.exp(upto(2 * pair + 1) - upto(2 * pair)), width)
    decay_second = spread(jnp.exp(upto(2 * pair + 2) - upto(2 * pair + 1)), width)
    ahead = (first_s * decay_second + second_s).astype(BF16)
    back = (first_p + second_p * decay_first).astype(BF16)
    s_sum = jnp.zeros_like(s_wide)
    p_sum = jnp.zeros_like(p_wide)
    for r in range(1, count // 2):
        ahead = lax.ppermute(ahead, "seq", [(i, i + 2) for i in range(count - 2)])
        back = lax.ppermute(back, "seq", [(i + 2, i) for i in range(count - 2)])
        w_ahead = jnp.exp(jnp.minimum(upto(2 * pair) - upto(2 * (pair - r) + 2), 0.0))
        w_back = jnp.exp(jnp.minimum(upto(2 * (pair + r)) - upto(2 * pair + 2), 0.0))
        s_sum = s_sum + ahead.astype(F32) * spread(w_ahead, width)
        p_sum = p_sum + back.astype(F32) * spread(w_back, width)
    state_in = jnp.where(odd == 1, s_sum * decay_first + first_s, s_sum)
    grad_in = jnp.where(odd == 1, p_sum, p_sum * decay_second + second_p)
    return state_in, grad_in


def per_device(
    ssd_input,
    log_decay,
    input_map,
    output_map,
    ssd_cotangent,
    queries,
    key_rows,
    value_rows,
    attn_cotangent,
    pair_order,
):
    count = lax.axis_size("seq")
    place = lax.axis_index("seq")
    rows, heads, width = ssd_input.shape
    groups, size = input_map.shape[1:]
    per = heads // groups
    span = per * width
    q_rows, q_heads, q_width = queries.shape
    half = q_rows // 2

    kv = lax.all_gather(
        jnp.concatenate([key_rows, value_rows], axis=1), "seq", axis=0, tiled=True
    )

    x = ssd_input.reshape(rows, heads * width)
    dy = ssd_cotangent.reshape(rows, heads * width)
    a = log_decay.reshape(rows, groups, per).transpose(1, 0, 2)
    a_t = a.transpose(0, 2, 1)
    b = input_map.reshape(rows, groups * size)
    c = output_map.reshape(rows, groups * size)

    wide_spec = pl.BlockSpec((rows, span), lambda g: (0, g))
    a_spec = pl.BlockSpec((1, rows, per), lambda g: (g, 0, 0))
    at_spec = pl.BlockSpec((1, per, rows), lambda g: (g, 0, 0))
    map_spec = pl.BlockSpec((rows, size), lambda g: (0, g))
    state_spec = pl.BlockSpec((1, size, span), lambda g: (g, 0, 0))
    state_flops = 4 * rows * heads * width * size
    s_own, p_own, tot = pl.pallas_call(
        state_kernel,
        grid=(groups,),
        in_specs=[wide_spec, wide_spec, a_spec, map_spec, map_spec],
        out_specs=[state_spec, state_spec, pl.BlockSpec((1, 1, per), lambda g: (g, 0, 0))],
        out_shape=[
            jax.ShapeDtypeStruct((groups, size, span), BF16),
            jax.ShapeDtypeStruct((groups, size, span), BF16),
            jax.ShapeDtypeStruct((groups, 1, per), F32),
        ],
        scratch_shapes=[pltpu.VMEM((rows, span), BF16), pltpu.VMEM((rows, span), BF16)],
        compiler_params=pltpu.CompilerParams(vmem_limit_bytes=VMEM_BYTES),
        cost_estimate=pl.CostEstimate(
            flops=state_flops, bytes_accessed=4 * rows * heads * width, transcendentals=0
        ),
    )(x, dy, a, b, c)

    state_in, grad_in = states_between(s_own, p_own, tot, width)

    blocks = 2 * count
    own_first = pair_order[place]
    own = jnp.stack([own_first, blocks - 1 - own_first]).astype(jnp.int32)
    ids = jnp.stack([pair_order, blocks - 1 - pair_order], axis=1).reshape(-1)
    block_ids = jnp.arange(blocks, dtype=jnp.int32)
    where_at = jnp.sum(
        jnp.where(ids[None, :] == block_ids[:, None], block_ids[None, :], 0), axis=1
    ).astype(jnp.int32)

    def by_half(array):
        parts = array.reshape(2, half, q_heads, q_width).transpose(0, 2, 1, 3)
        return parts.reshape(2, q_heads * half, q_width)

    vmem = pl.BlockSpec(memory_space=pltpu.VMEM)
    smem = pl.BlockSpec(memory_space=pltpu.SMEM)
    quarters = lax.axis_size("head")
    lanes_q = q_heads * half
    dq, dkv = pl.pallas_call(
        attention_kernel,
        in_specs=[smem, smem, vmem, vmem, vmem],
        out_specs=[vmem, vmem],
        out_shape=[
            jax.ShapeDtypeStruct((2, lanes_q, q_width), BF16),
            jax.ShapeDtypeStruct((quarters, count, q_rows // quarters, 2 * q_width), BF16),
        ],
        scratch_shapes=[
            pltpu.VMEM((blocks, half, lanes_q), F32),
            pltpu.VMEM((blocks, half, lanes_q), BF16),
            pltpu.VMEM((count * q_rows, 2 * q_width), F32),
        ],
        compiler_params=pltpu.CompilerParams(vmem_limit_bytes=VMEM_BYTES),
        cost_estimate=pl.CostEstimate(
            flops=12 * (blocks + 1) * half * lanes_q * q_width,
            bytes_accessed=4 * count * q_rows * q_width * 4,
            transcendentals=(blocks + 1) * half * lanes_q,
        ),
    )(where_at, own, by_half(queries), by_half(attn_cotangent), kv)

    dkv = lax.psum_scatter(dkv, "head", scatter_dimension=0, tiled=True)[0]
    dkv = lax.psum_scatter(dkv, "seq", scatter_dimension=0, tiled=True)[0]
    dkv = lax.all_gather(dkv, "head", axis=0, tiled=True)
    grad_keys = dkv[:, :q_width]
    grad_values = dkv[:, q_width:]
    grad_queries = (
        dq.reshape(2, q_heads, half, q_width).transpose(0, 2, 1, 3).reshape(queries.shape)
    )

    dx, da, db, dc = pl.pallas_call(
        scan_kernel,
        grid=(groups,),
        in_specs=[
            wide_spec,
            wide_spec,
            a_spec,
            at_spec,
            map_spec,
            map_spec,
            state_spec,
            state_spec,
        ],
        out_specs=[wide_spec, a_spec, map_spec, map_spec],
        out_shape=[
            jax.ShapeDtypeStruct((rows, heads * width), BF16),
            jax.ShapeDtypeStruct((groups, rows, per), F32),
            jax.ShapeDtypeStruct((rows, groups * size), F32),
            jax.ShapeDtypeStruct((rows, groups * size), F32),
        ],
        scratch_shapes=[
            pltpu.VMEM((rows // BLOCK, size, span), BF16),
            pltpu.VMEM((rows, span), BF16),
            pltpu.VMEM((BLOCK, span), BF16),
            pltpu.VMEM((size, span), F32),
            pltpu.VMEM((size, span), F32),
            pltpu.VMEM((BLOCK, BLOCK), F32),
        ],
        compiler_params=pltpu.CompilerParams(vmem_limit_bytes=VMEM_BYTES),
        cost_estimate=pl.CostEstimate(
            flops=5 * state_flops,
            bytes_accessed=8 * rows * heads * width,
            transcendentals=rows * heads * BLOCK,
        ),
    )(x, dy, a, a_t, b, c, state_in, grad_in)

    return (
        dx.reshape(rows, heads, width),
        da.transpose(1, 0, 2).reshape(rows, heads),
        db.reshape(rows, groups, size),
        dc.reshape(rows, groups, size),
        grad_queries,
        grad_keys,
        grad_values,
    )


def solution(mesh):
    return jax.shard_map(
        per_device,
        mesh=mesh,
        in_specs=(
            P("seq", "head", None),
            P("seq", "head"),
            P("seq", "head", None),
            P("seq", "head", None),
            P("seq", "head", None),
            P("seq", "head", None),
            P("seq", None),
            P("seq", None),
            P("seq", "head", None),
            P(),
        ),
        out_specs=(
            P("seq", "head", None),
            P("seq", "head"),
            P("seq", "head", None),
            P("seq", "head", None),
            P("seq", "head", None),
            P("seq", None),
            P("seq", None),
        ),
        check_vma=False,
    )
```

```python
import functools
import math

import jax
import jax.numpy as jnp
from jax import lax
from jax.experimental import pallas as pl
from jax.experimental.pallas import tpu as pltpu
from jax.sharding import PartitionSpec as P

BLOCK = 128
HIGHEST = lax.Precision.HIGHEST
NEG_FILL = -1e30
F32 = jnp.float32
BF16 = jnp.bfloat16
VMEM_BYTES = 52 * 1024 * 1024


def dot(a, b):
    return jnp.dot(a, b, preferred_element_type=F32)


def dot_t(a, b):
    return lax.dot_general(a, b, (((1,), (1,)), ((), ())), preferred_element_type=F32)


def dot_hi(a, b):
    return jnp.dot(a, b, preferred_element_type=F32, precision=HIGHEST)


def iota2(shape, dim):
    return lax.broadcasted_iota(jnp.int32, shape, dim)


def lower_ones():
    shape = (BLOCK, BLOCK)
    return (iota2(shape, 0) >= iota2(shape, 1)).astype(F32)


def upper_ones():
    shape = (BLOCK, BLOCK)
    return (iota2(shape, 0) <= iota2(shape, 1)).astype(F32)


def state_kernel(x_ref, dy_ref, a_ref, b_ref, c_ref, sp_ref, tx, ey):
    rows, heads = a_ref.shape[1:]
    width = x_ref.shape[1] // heads
    lower = lower_ones()
    offset = jnp.zeros((1, heads), F32)
    cums = []
    for k in range(rows // BLOCK):
        cum = dot_hi(lower, a_ref[0, pl.ds(k * BLOCK, BLOCK), :])
        cums.append(cum + offset)
        offset = offset + cum[BLOCK - 1 :, :]
    for k, cum in enumerate(cums):
        span = pl.ds(k * BLOCK, BLOCK)
        tail = jnp.exp(offset - cum)
        head_decay = jnp.exp(cum)
        for h in range(heads):
            lanes = pl.ds(h * width, width)
            tx[span, lanes] = (x_ref[span, lanes].astype(F32) * tail[:, h : h + 1]).astype(BF16)
            ey[span, lanes] = (
                dy_ref[span, lanes].astype(F32) * head_decay[:, h : h + 1]
            ).astype(BF16)
    b_t = b_ref[0].T.astype(BF16)
    c_t = c_ref[0].T.astype(BF16)
    chunks, _, _, step = sp_ref.shape
    for at in range(chunks):
        lanes = pl.ds(at * step, step)
        sp_ref[at, 0] = dot(b_t, tx[:, lanes]).astype(BF16)
        sp_ref[at, 1] = dot(c_t, ey[:, lanes]).astype(BF16)


def scan_kernel(
    pairs,
    x_ref,
    dy_ref,
    a_ref,
    at_ref,
    b_ref,
    c_ref,
    sp_ref,
    w_ref,
    dx_ref,
    da_ref,
    db_ref,
    dc_ref,
    y_in,
    f_in,
    b_in,
    f_out,
    b_out,
    states,
    tails,
    s_all,
    ds_all,
    gts,
    dgt,
    maps_low,
    maps_t,
    y_send,
    y_recv,
    f_send,
    f_recv,
    b_send,
    b_recv,
):
    chunks, rows, heads = a_ref.shape
    groups, _, size = b_ref.shape
    per_group = chunks // groups
    width = x_ref.shape[1] // (chunks * heads)
    count = rows // BLOCK
    me = lax.axis_index("seq")
    pair = me // 2
    odd = me - 2 * pair
    partner = me + 1 - 2 * odd
    up = me + 2
    down = me - 2
    has_up = pair < pairs - 1
    has_down = pair > 0

    barrier = pltpu.get_barrier_semaphore()

    def greet(device):
        pl.semaphore_signal(
            barrier, inc=1, device_id={"seq": device}, device_id_type=pl.DeviceIdType.MESH
        )

    greet(partner)
    pl.when(has_up)(lambda: greet(up))
    pl.when(has_down)(lambda: greet(down))
    pl.semaphore_wait(barrier, 1 + has_up.astype(jnp.int32) + has_down.astype(jnp.int32))

    def remote(src, dst, send, recv, c, device):
        return pltpu.make_async_remote_copy(
            src_ref=src.at[c],
            dst_ref=dst.at[c],
            send_sem=send.at[c],
            recv_sem=recv.at[c],
            device_id={"seq": device},
            device_id_type=pl.DeviceIdType.MESH,
        )

    def swap(c):
        return remote(sp_ref, y_in, y_send, y_recv, c, partner)

    def climb(c):
        return remote(f_out, f_in, f_send, f_recv, c, up)

    def descend(c):
        return remote(b_out, b_in, b_send, b_recv, c, down)

    ahead = min(2, chunks)
    for c in range(ahead):
        swap(c).start()

    lower = lower_ones()
    upper = upper_ones()
    causal = iota2((BLOCK, BLOCK), 0) <= iota2((BLOCK, BLOCK), 1)
    db_ref[...] = jnp.zeros_like(db_ref)
    dc_ref[...] = jnp.zeros_like(dc_ref)
    dgt[...] = jnp.zeros_like(dgt)

    def prepare(at, carry):
        g = at // count
        span = pl.ds(pl.multiple_of((at - g * count) * BLOCK, BLOCK), BLOCK)
        b_wide = b_ref[g, span, :]
        c_wide = c_ref[g, span, :]
        gts[at] = lax.dot_general(
            b_wide, c_wide, (((1,), (1,)), ((), ())), preferred_element_type=F32, precision=HIGHEST
        )
        maps_low[at, 0] = b_wide.astype(BF16)
        maps_low[at, 1] = c_wide.astype(BF16)
        maps_t[at, 0] = b_wide.T.astype(BF16)
        maps_t[at, 1] = c_wide.T.astype(BF16)
        return carry

    lax.fori_loop(0, groups * count, prepare, 0)
    is_odd = odd == 1

    def forward_link(c):
        own = sp_ref[c, 0].astype(F32)
        other = y_in[c, 0].astype(F32)
        first = jnp.where(is_odd, other, own)
        second = jnp.where(is_odd, own, other)
        w_first = w_ref[c, 0:1, :]
        w_second = w_ref[c, 1:2, :]
        f_out[c] = (first * w_second + second).astype(BF16)
        s_all[c] = jnp.where(is_odd, first, 0.0)

        @pl.when(has_down)
        def _():
            climb(c).wait_recv()
            arrived = f_in[c].astype(F32)
            s_all[c] = jnp.where(is_odd, arrived * w_first + first, arrived)
            total = first * w_second + second + arrived * (w_first * w_second)
            f_out[c] = total.astype(BF16)

        pl.when(has_up)(lambda: climb(c).start())

    def backward_link(c):
        own = sp_ref[c, 1].astype(F32)
        other = y_in[c, 1].astype(F32)
        first = jnp.where(is_odd, other, own)
        second = jnp.where(is_odd, own, other)
        w_first = w_ref[c, 0:1, :]
        w_second = w_ref[c, 1:2, :]
        b_out[c] = (first + second * w_first).astype(BF16)
        ds_all[c] = jnp.where(is_odd, 0.0, second)

        @pl.when(has_up)
        def _():
            descend(c).wait_recv()
            arrived = b_in[c].astype(F32)
            ds_all[c] = jnp.where(is_odd, arrived, arrived * w_second + second)
            total = first + second * w_first + arrived * (w_first * w_second)
            b_out[c] = total.astype(BF16)

        pl.when(has_down)(lambda: descend(c).start())

    def scan_chunk(c):
        g = c // per_group
        base = c * (heads * width)

        def lanes_of(h):
            return pl.ds(pl.multiple_of(base + h * width, width), width)

        def forward(k, carry):
            span = pl.ds(pl.multiple_of(k * BLOCK, BLOCK), BLOCK)
            cum = dot_hi(lower, a_ref[c, span, :])
            last = cum[BLOCK - 1 :, :]
            tail = jnp.exp(last - cum)
            whole = jnp.exp(last)
            b_t = maps_t[g * count + k, 0]
            for h in range(heads):
                lanes = pl.ds(h * width, width)
                tail_x = (x_ref[span, lanes_of(h)].astype(F32) * tail[:, h : h + 1]).astype(BF16)
                tails[span, lanes] = tail_x
                now = s_all[c, :, lanes]
                states[k, :, lanes] = now.astype(BF16)
                s_all[c, :, lanes] = now * whole[:, h : h + 1] + dot(b_t, tail_x)
            return carry

        lax.fori_loop(0, count, forward, 0)

        def backward(turn, carry):
            k = count - 1 - turn
            at = g * count + k
            span = pl.ds(pl.multiple_of(k * BLOCK, BLOCK), BLOCK)
            cum = dot_hi(lower, a_ref[c, span, :])
            cum_t = dot_hi(at_ref[c, :, span], upper)
            last = cum[BLOCK - 1 :, :]
            tail = jnp.exp(last - cum)
            whole = jnp.exp(last)
            grow = jnp.exp(cum)
            b_low = maps_low[at, 0]
            c_low = maps_low[at, 1]
            c_t = maps_t[at, 1]
            gt = gts[at]
            columns = jnp.zeros((BLOCK, heads), F32)
            row_sums = jnp.zeros((heads, BLOCK), F32)
            totals = jnp.zeros((heads, BLOCK), F32)
            column_at = iota2((BLOCK, heads), 1)
            row_at = iota2((heads, BLOCK), 0)
            db = jnp.zeros((BLOCK, size), F32)
            dc = jnp.zeros((BLOCK, size), F32)
            dg = jnp.zeros((BLOCK, BLOCK), F32)
            for h in range(heads):
                lanes = pl.ds(h * width, width)
                x_h = x_ref[span, lanes_of(h)]
                dy_h = dy_ref[span, lanes_of(h)]
                tail_x = tails[span, lanes]
                state = states[k, :, lanes]
                ds_wide = ds_all[c, :, lanes]
                ds_low = ds_wide.astype(BF16)
                decay = jnp.exp(
                    jnp.where(causal, cum_t[h : h + 1, :] - cum[:, h : h + 1], NEG_FILL)
                )
                t1 = dot_t(x_h, dy_h) * decay
                dg = dg + t1
                mt = t1 * gt
                from_state = dot(b_low, ds_low)
                dx = dot((gt * decay).astype(BF16), dy_h) + from_state * tail[:, h : h + 1]
                dx_ref[span, lanes_of(h)] = dx.astype(BF16)
                edy_h = (dy_h.astype(F32) * grow[:, h : h + 1]).astype(BF16)
                r2 = tail_x.astype(F32) * from_state
                column = jnp.sum(
                    edy_h.astype(F32) * dot(c_low, state) - r2 - mt, axis=1, keepdims=True
                )
                columns = jnp.where(column_at == h, column, columns)
                row_sums = jnp.where(row_at == h, jnp.sum(mt, axis=0, keepdims=True), row_sums)
                total = jnp.sum(r2, axis=0, keepdims=True) + whole[:, h : h + 1] * jnp.sum(
                    ds_wide * state.astype(F32), axis=0, keepdims=True
                )
                totals = jnp.where(row_at == h, total, totals)
                dc = dc + dot_t(edy_h, state)
                db = db + dot_t(tail_x, ds_low)
                ds_all[c, :, lanes] = ds_wide * whole[:, h : h + 1] + dot(c_t, edy_h)
            dgt[at] += dg
            db_ref[g, span, :] += db
            dc_ref[g, span, :] += dc
            total = jnp.sum(totals, axis=1, keepdims=True)
            row_sums = row_sums + jnp.where(iota2((heads, BLOCK), 1) == BLOCK - 1, total, 0.0)
            da_ref[c, span, :] = dot_hi(upper, columns + row_sums.T)
            return carry

        lax.fori_loop(0, count, backward, 0)

    def turn(t, carry):
        @pl.when(t < chunks)
        def _():
            swap(t).wait_recv()

        @pl.when(t + ahead < chunks)
        def _():
            swap(t + ahead).start()

        cf = t - pair

        @pl.when((cf >= 0) & (cf < chunks))
        def _():
            forward_link(cf)

        cb = t - (pairs - 1 - pair)

        @pl.when((cb >= 0) & (cb < chunks))
        def _():
            backward_link(cb)

        done = t - (pairs - 1)

        @pl.when(done >= 0)
        def _():
            scan_chunk(done)

        return carry

    lax.fori_loop(0, chunks + pairs - 1, turn, 0)

    def finish(at, carry):
        g = at // count
        span = pl.ds(pl.multiple_of((at - g * count) * BLOCK, BLOCK), BLOCK)
        dg = dgt[at]
        db_ref[g, span, :] += dot_hi(dg, c_ref[g, span, :])
        dc_ref[g, span, :] += dot_hi(dg.T, b_ref[g, span, :])
        return carry

    lax.fori_loop(0, groups * count, finish, 0)

    def settle(c, carry):
        swap(c).wait_send()
        pl.when(has_up)(lambda: climb(c).wait_send())
        pl.when(has_down)(lambda: descend(c).wait_send())
        return carry

    lax.fori_loop(0, chunks, settle, 0)


def attention_kernel(
    place_ref, own_ref, q_ref, do_ref, kv_ref, dq_ref, dkv_ref, scores, probs, acc
):
    halves, lanes_q, width = q_ref.shape
    half = kv_ref.shape[0] // place_ref.shape[0]
    scale = width ** (-0.5)
    rate = scale * math.log2(math.e)
    acc[...] = jnp.zeros_like(acc)
    visible = iota2((half, lanes_q), 0) <= lax.rem(iota2((half, lanes_q), 1), half)

    def rows_of(j):
        return pl.ds(pl.multiple_of(place_ref[j] * half, half), half)

    def fold(op, tile):
        return op(tile.reshape(half // 8, 8, lanes_q), axis=0)

    for i in range(halves):
        own = own_ref[i]
        q = q_ref[i]
        q_t = q.T

        def score(j):
            return dot(kv_ref[rows_of(j), :width], q_t)

        def first(j, top):
            tile = score(j)
            scores[j] = tile
            return jnp.maximum(top, fold(jnp.max, tile))

        tile = jnp.where(visible, score(own), NEG_FILL)
        scores[own] = tile
        top = lax.fori_loop(0, own, first, fold(jnp.max, tile))
        top = jnp.max(top, axis=0, keepdims=True) * rate

        def second(j, carry):
            sums, out_t = carry
            prob = jnp.exp2(scores[j] * rate - top)
            low = prob.astype(BF16)
            probs[j] = low
            value_t = kv_ref[rows_of(j), width:].T
            return (sums + fold(jnp.sum, prob), out_t + dot(value_t, low))

        sums, out_t = lax.fori_loop(
            0,
            own + 1,
            second,
            (jnp.zeros((8, lanes_q), F32), jnp.zeros((width, lanes_q), F32)),
        )
        inverse = 1.0 / jnp.sum(sums, axis=0, keepdims=True)
        do_t = do_ref[i].astype(F32).T
        out_low = (out_t * inverse).astype(BF16).astype(F32)
        delta = jnp.sum(do_t * out_low, axis=0, keepdims=True) * inverse
        do_scaled = do_t * inverse
        do_t_low = do_scaled.astype(BF16)
        do_low = do_scaled.T.astype(BF16)

        def third(j, dq_t):
            at = rows_of(j)
            key = kv_ref[at, :width]
            prob = probs[j]
            prob_grad = dot(kv_ref[at, width:], do_t_low)
            ds = (prob.astype(F32) * (prob_grad - delta)).astype(BF16)
            acc[at, :width] += dot(ds, q)
            acc[at, width:] += dot(prob, do_low)
            return dq_t + dot(key.T, ds)

        dq_t = lax.fori_loop(0, own + 1, third, jnp.zeros((width, lanes_q), F32))
        dq_ref[i] = (dq_t * scale).T.astype(BF16)

    quarters, devices, rows = dkv_ref.shape[:3]
    for d in range(devices):
        for u in range(quarters):
            span = pl.ds((d * quarters + u) * rows, rows)
            dkv_ref[u, d, :, :width] = (acc[span, :width] * scale).astype(BF16)
            dkv_ref[u, d, :, width:] = acc[span, width:].astype(BF16)


def pair_decays(log_decay, chunks, width):
    pair = lax.axis_index("seq") // 2
    tots = lax.all_gather(jnp.sum(log_decay, axis=0, keepdims=True), "seq")
    own = lax.dynamic_slice_in_dim(tots[:, 0], 2 * pair, 2, 0)
    decays = jnp.repeat(jnp.exp(own), width, axis=1)
    return decays.reshape(2, chunks, -1).transpose(1, 0, 2)


def per_device(
    ssd_input,
    log_decay,
    input_map,
    output_map,
    ssd_cotangent,
    queries,
    key_rows,
    value_rows,
    attn_cotangent,
    pair_order,
):
    count = lax.axis_size("seq")
    place = lax.axis_index("seq")
    rows, heads, width = ssd_input.shape
    groups, size = input_map.shape[1:]
    per = heads // groups
    span = per * width
    q_rows, q_heads, q_width = queries.shape
    half = q_rows // 2

    kv = lax.all_gather(
        jnp.concatenate([key_rows, value_rows], axis=1), "seq", axis=0, tiled=True
    )

    chunk = min(4, per)
    chunks = heads // chunk
    per_chunks = per // chunk
    step = chunk * width
    decays = pair_decays(log_decay, chunks, width)
    x = ssd_input.reshape(rows, heads * width)
    dy = ssd_cotangent.reshape(rows, heads * width)
    a = log_decay.reshape(rows, groups, per).transpose(1, 0, 2)
    a_chunks = log_decay.reshape(rows, chunks, chunk).transpose(1, 0, 2)
    a_t = a_chunks.transpose(0, 2, 1)
    b = input_map.transpose(1, 0, 2)
    c = output_map.transpose(1, 0, 2)

    wide_spec = pl.BlockSpec((rows, span), lambda g: (0, g))
    a_spec = pl.BlockSpec((1, rows, per), lambda g: (g, 0, 0))
    map_spec = pl.BlockSpec((1, rows, size), lambda g: (g, 0, 0))
    state_flops = 4 * rows * heads * width * size
    sp = pl.pallas_call(
        state_kernel,
        grid=(groups,),
        in_specs=[wide_spec, wide_spec, a_spec, map_spec, map_spec],
        out_specs=pl.BlockSpec((per_chunks, 2, size, step), lambda g: (g, 0, 0, 0)),
        out_shape=jax.ShapeDtypeStruct((chunks, 2, size, step), BF16),
        scratch_shapes=[pltpu.VMEM((rows, span), BF16), pltpu.VMEM((rows, span), BF16)],
        compiler_params=pltpu.CompilerParams(vmem_limit_bytes=VMEM_BYTES),
        cost_estimate=pl.CostEstimate(
            flops=state_flops, bytes_accessed=4 * rows * heads * width, transcendentals=0
        ),
    )(x, dy, a, b, c)

    blocks = 2 * count
    own_first = pair_order[place]
    own = jnp.stack([own_first, blocks - 1 - own_first]).astype(jnp.int32)
    ids = jnp.stack([pair_order, blocks - 1 - pair_order], axis=1).reshape(-1)
    block_ids = jnp.arange(blocks, dtype=jnp.int32)
    where_at = jnp.sum(
        jnp.where(ids[None, :] == block_ids[:, None], block_ids[None, :], 0), axis=1
    ).astype(jnp.int32)

    def by_half(array):
        parts = array.reshape(2, half, q_heads, q_width).transpose(0, 2, 1, 3)
        return parts.reshape(2, q_heads * half, q_width)

    vmem = pl.BlockSpec(memory_space=pltpu.VMEM)
    smem = pl.BlockSpec(memory_space=pltpu.SMEM)
    quarters = lax.axis_size("head")
    lanes_q = q_heads * half
    dq, dkv = pl.pallas_call(
        attention_kernel,
        in_specs=[smem, smem, vmem, vmem, vmem],
        out_specs=[vmem, vmem],
        out_shape=[
            jax.ShapeDtypeStruct((2, lanes_q, q_width), BF16),
            jax.ShapeDtypeStruct((quarters, count, q_rows // quarters, 2 * q_width), BF16),
        ],
        scratch_shapes=[
            pltpu.VMEM((blocks, half, lanes_q), F32),
            pltpu.VMEM((blocks, half, lanes_q), BF16),
            pltpu.VMEM((count * q_rows, 2 * q_width), F32),
        ],
        compiler_params=pltpu.CompilerParams(vmem_limit_bytes=VMEM_BYTES),
        cost_estimate=pl.CostEstimate(
            flops=12 * (blocks + 1) * half * lanes_q * q_width,
            bytes_accessed=4 * count * q_rows * q_width * 4,
            transcendentals=(blocks + 1) * half * lanes_q,
        ),
    )(where_at, own, by_half(queries), by_half(attn_cotangent), kv)

    sp, dkv = lax.optimization_barrier((sp, dkv))
    dkv = lax.psum_scatter(dkv, "head", scatter_dimension=0, tiled=True)[0]
    dkv = lax.psum_scatter(dkv, "seq", scatter_dimension=0, tiled=True)[0]
    dkv = lax.all_gather(dkv, "head", axis=0, tiled=True)
    grad_keys = dkv[:, :q_width]
    grad_values = dkv[:, q_width:]
    grad_queries = (
        dq.reshape(2, q_heads, half, q_width).transpose(0, 2, 1, 3).reshape(queries.shape)
    )

    pairs = count // 2
    parts = rows // BLOCK
    sems = [pltpu.SemaphoreType.DMA((chunks,)) for _ in range(6)]
    dx, da, db, dc = pl.pallas_call(
        functools.partial(scan_kernel, pairs),
        in_specs=[vmem] * 8,
        out_specs=[vmem] * 4,
        out_shape=[
            jax.ShapeDtypeStruct((rows, heads * width), BF16),
            jax.ShapeDtypeStruct((chunks, rows, chunk), F32),
            jax.ShapeDtypeStruct((groups, rows, size), F32),
            jax.ShapeDtypeStruct((groups, rows, size), F32),
        ],
        scratch_shapes=[
            pltpu.VMEM((chunks, 2, size, step), BF16),
            pltpu.VMEM((chunks, size, step), BF16),
            pltpu.VMEM((chunks, size, step), BF16),
            pltpu.VMEM((chunks, size, step), BF16),
            pltpu.VMEM((chunks, size, step), BF16),
            pltpu.VMEM((parts, size, step), BF16),
            pltpu.VMEM((rows, step), BF16),
            pltpu.VMEM((chunks, size, step), F32),
            pltpu.VMEM((chunks, size, step), F32),
            pltpu.VMEM((groups * parts, BLOCK, BLOCK), F32),
            pltpu.VMEM((groups * parts, BLOCK, BLOCK), F32),
            pltpu.VMEM((groups * parts, 2, BLOCK, size), BF16),
            pltpu.VMEM((groups * parts, 2, size, BLOCK), BF16),
            *sems,
        ],
        compiler_params=pltpu.CompilerParams(
            vmem_limit_bytes=VMEM_BYTES, collective_id=0, has_side_effects=True
        ),
        cost_estimate=pl.CostEstimate(
            flops=5 * state_flops,
            bytes_accessed=8 * rows * heads * width,
            transcendentals=rows * heads * BLOCK,
        ),
    )(x, dy, a_chunks, a_t, b, c, sp, decays)

    return (
        dx.reshape(rows, heads, width),
        da.transpose(1, 0, 2).reshape(rows, heads),
        db.transpose(1, 0, 2),
        dc.transpose(1, 0, 2),
        grad_queries,
        grad_keys,
        grad_values,
    )


def solution(mesh):
    return jax.shard_map(
        per_device,
        mesh=mesh,
        in_specs=(
            P("seq", "head", None),
            P("seq", "head"),
            P("seq", "head", None),
            P("seq", "head", None),
            P("seq", "head", None),
            P("seq", "head", None),
            P("seq", None),
            P("seq", None),
            P("seq", "head", None),
            P(),
        ),
        out_specs=(
            P("seq", "head", None),
            P("seq", "head"),
            P("seq", "head", None),
            P("seq", "head", None),
            P("seq", "head", None),
            P("seq", None),
            P("seq", None),
        ),
        check_vma=False,
    )
```

```python
import functools
import math

import jax
import jax.numpy as jnp
from jax import lax
from jax.experimental import pallas as pl
from jax.experimental.pallas import tpu as pltpu
from jax.sharding import PartitionSpec as P

BLOCK = 128
HIGHEST = lax.Precision.HIGHEST
NEG_FILL = -1e30
F32 = jnp.float32
BF16 = jnp.bfloat16
VMEM_BYTES = 52 * 1024 * 1024


def dot(a, b):
    return jnp.dot(a, b, preferred_element_type=F32)


def dot_t(a, b):
    return lax.dot_general(a, b, (((1,), (1,)), ((), ())), preferred_element_type=F32)


def dot_hi(a, b):
    return jnp.dot(a, b, preferred_element_type=F32, precision=HIGHEST)


def iota2(shape, dim):
    return lax.broadcasted_iota(jnp.int32, shape, dim)


def lower_ones():
    shape = (BLOCK, BLOCK)
    return (iota2(shape, 0) >= iota2(shape, 1)).astype(F32)


def upper_ones():
    shape = (BLOCK, BLOCK)
    return (iota2(shape, 0) <= iota2(shape, 1)).astype(F32)


def state_kernel(x_ref, dy_ref, a_ref, b_ref, c_ref, sp_ref, tx, ey):
    rows, heads = a_ref.shape[1:]
    width = x_ref.shape[1] // heads
    lower = lower_ones()
    offset = jnp.zeros((1, heads), F32)
    cums = []
    for k in range(rows // BLOCK):
        cum = dot_hi(lower, a_ref[0, pl.ds(k * BLOCK, BLOCK), :])
        cums.append(cum + offset)
        offset = offset + cum[BLOCK - 1 :, :]
    for k, cum in enumerate(cums):
        span = pl.ds(k * BLOCK, BLOCK)
        tail = jnp.exp(offset - cum)
        head_decay = jnp.exp(cum)
        for h in range(heads):
            lanes = pl.ds(h * width, width)
            tx[span, lanes] = (x_ref[span, lanes].astype(F32) * tail[:, h : h + 1]).astype(BF16)
            ey[span, lanes] = (
                dy_ref[span, lanes].astype(F32) * head_decay[:, h : h + 1]
            ).astype(BF16)
    b_t = b_ref[0].T.astype(BF16)
    c_t = c_ref[0].T.astype(BF16)
    chunks, _, _, step = sp_ref.shape
    for at in range(chunks):
        lanes = pl.ds(at * step, step)
        sp_ref[at, 0] = dot(b_t, tx[:, lanes]).astype(BF16)
        sp_ref[at, 1] = dot(c_t, ey[:, lanes]).astype(BF16)


def scan_kernel(
    pairs,
    x_ref,
    dy_ref,
    a_ref,
    at_ref,
    b_ref,
    c_ref,
    sp_ref,
    w_ref,
    dx_ref,
    da_ref,
    db_ref,
    dc_ref,
    y_in,
    f_in,
    b_in,
    f_out,
    b_out,
    states,
    tails,
    s_all,
    ds_all,
    gts,
    dgt,
    maps_low,
    maps_t,
    cums,
    cums_t,
    y_send,
    y_recv,
    f_send,
    f_recv,
    b_send,
    b_recv,
):
    chunks = sp_ref.shape[0]
    rows, all_heads = a_ref.shape
    heads = all_heads // chunks
    groups, _, size = b_ref.shape
    per_group = chunks // groups
    width = x_ref.shape[1] // (chunks * heads)
    count = rows // BLOCK
    me = lax.axis_index("seq")
    pair = me // 2
    odd = me - 2 * pair
    partner = me + 1 - 2 * odd
    up = me + 2
    down = me - 2
    has_up = pair < pairs - 1
    has_down = pair > 0

    barrier = pltpu.get_barrier_semaphore()

    def greet(device):
        pl.semaphore_signal(
            barrier, inc=1, device_id={"seq": device}, device_id_type=pl.DeviceIdType.MESH
        )

    greet(partner)
    pl.when(has_up)(lambda: greet(up))
    pl.when(has_down)(lambda: greet(down))
    pl.semaphore_wait(barrier, 1 + has_up.astype(jnp.int32) + has_down.astype(jnp.int32))

    def remote(src, dst, send, recv, c, device):
        return pltpu.make_async_remote_copy(
            src_ref=src.at[c],
            dst_ref=dst.at[c],
            send_sem=send.at[c],
            recv_sem=recv.at[c],
            device_id={"seq": device},
            device_id_type=pl.DeviceIdType.MESH,
        )

    def swap(c):
        return remote(sp_ref, y_in, y_send, y_recv, c, partner)

    def climb(c):
        return remote(f_out, f_in, f_send, f_recv, c, up)

    def descend(c):
        return remote(b_out, b_in, b_send, b_recv, c, down)

    ahead = min(2, chunks)
    for c in range(ahead):
        swap(c).start()

    lower = lower_ones()
    upper = upper_ones()
    causal = iota2((BLOCK, BLOCK), 0) <= iota2((BLOCK, BLOCK), 1)
    db_ref[...] = jnp.zeros_like(db_ref)
    dc_ref[...] = jnp.zeros_like(dc_ref)
    dgt[...] = jnp.zeros_like(dgt)
    da_ref[...] = jnp.zeros_like(da_ref)
    for k in range(count):
        span = pl.ds(k * BLOCK, BLOCK)
        cum = dot_hi(lower, a_ref[span, :])
        cum_t = dot_hi(at_ref[:, span], upper)
        for c in range(chunks):
            cums[c, span, :] = cum[:, c * heads : (c + 1) * heads]
            cums_t[c, :, span] = cum_t[c * heads : (c + 1) * heads, :]

    def prepare(at, carry):
        g = at // count
        span = pl.ds(pl.multiple_of((at - g * count) * BLOCK, BLOCK), BLOCK)
        b_wide = b_ref[g, span, :]
        c_wide = c_ref[g, span, :]
        gts[at] = lax.dot_general(
            b_wide, c_wide, (((1,), (1,)), ((), ())), preferred_element_type=F32, precision=HIGHEST
        )
        maps_low[at, 0] = b_wide.astype(BF16)
        maps_low[at, 1] = c_wide.astype(BF16)
        maps_t[at, 0] = b_wide.T.astype(BF16)
        maps_t[at, 1] = c_wide.T.astype(BF16)
        return carry

    lax.fori_loop(0, groups * count, prepare, 0)
    is_odd = odd == 1

    def forward_link(c):
        own = sp_ref[c, 0].astype(F32)
        other = y_in[c, 0].astype(F32)
        first = jnp.where(is_odd, other, own)
        second = jnp.where(is_odd, own, other)
        w_first = w_ref[c, 0:1, :]
        w_second = w_ref[c, 1:2, :]
        f_out[c] = (first * w_second + second).astype(BF16)
        s_all[c] = jnp.where(is_odd, first, 0.0)

        @pl.when(has_down)
        def _():
            climb(c).wait_recv()
            arrived = f_in[c].astype(F32)
            s_all[c] = jnp.where(is_odd, arrived * w_first + first, arrived)
            total = first * w_second + second + arrived * (w_first * w_second)
            f_out[c] = total.astype(BF16)

        pl.when(has_up)(lambda: climb(c).start())

    def backward_link(c):
        own = sp_ref[c, 1].astype(F32)
        other = y_in[c, 1].astype(F32)
        first = jnp.where(is_odd, other, own)
        second = jnp.where(is_odd, own, other)
        w_first = w_ref[c, 0:1, :]
        w_second = w_ref[c, 1:2, :]
        b_out[c] = (first + second * w_first).astype(BF16)
        ds_all[c] = jnp.where(is_odd, 0.0, second)

        @pl.when(has_up)
        def _():
            descend(c).wait_recv()
            arrived = b_in[c].astype(F32)
            ds_all[c] = jnp.where(is_odd, arrived, arrived * w_second + second)
            total = first + second * w_first + arrived * (w_first * w_second)
            b_out[c] = total.astype(BF16)

        pl.when(has_down)(lambda: descend(c).start())

    def scan_chunk(c):
        g = c // per_group
        base = c * (heads * width)

        def lanes_of(h):
            return pl.ds(pl.multiple_of(base + h * width, width), width)

        def forward(k, carry):
            span = pl.ds(pl.multiple_of(k * BLOCK, BLOCK), BLOCK)
            cum = cums[c, span, :]
            last = cum[BLOCK - 1 :, :]
            tail = jnp.exp(last - cum)
            whole = jnp.exp(last)
            b_t = maps_t[g * count + k, 0]
            for h in range(heads):
                lanes = pl.ds(h * width, width)
                tail_x = (x_ref[span, lanes_of(h)].astype(F32) * tail[:, h : h + 1]).astype(BF16)
                tails[span, lanes] = tail_x
                now = s_all[c, :, lanes]
                states[k, :, lanes] = now.astype(BF16)
                s_all[c, :, lanes] = now * whole[:, h : h + 1] + dot(b_t, tail_x)
            return carry

        lax.fori_loop(0, count, forward, 0)

        def backward(turn, carry):
            k = count - 1 - turn
            at = g * count + k
            span = pl.ds(pl.multiple_of(k * BLOCK, BLOCK), BLOCK)
            cum = cums[c, span, :]
            cum_t = cums_t[c, :, span]
            last = cum[BLOCK - 1 :, :]
            tail = jnp.exp(last - cum)
            whole = jnp.exp(last)
            grow = jnp.exp(cum)
            b_low = maps_low[at, 0]
            c_low = maps_low[at, 1]
            c_t = maps_t[at, 1]
            gt = gts[at]
            columns = jnp.zeros((BLOCK, all_heads), F32)
            row_sums = jnp.zeros((all_heads, BLOCK), F32)
            totals = jnp.zeros((all_heads, BLOCK), F32)
            column_at = iota2((BLOCK, all_heads), 1) - c * heads
            row_at = iota2((all_heads, BLOCK), 0) - c * heads
            db = jnp.zeros((BLOCK, size), F32)
            dc = jnp.zeros((BLOCK, size), F32)
            dg = jnp.zeros((BLOCK, BLOCK), F32)
            for h in range(heads):
                lanes = pl.ds(h * width, width)
                x_h = x_ref[span, lanes_of(h)]
                dy_h = dy_ref[span, lanes_of(h)]
                tail_x = tails[span, lanes]
                state = states[k, :, lanes]
                ds_wide = ds_all[c, :, lanes]
                ds_low = ds_wide.astype(BF16)
                decay = jnp.exp(
                    jnp.where(causal, cum_t[h : h + 1, :] - cum[:, h : h + 1], NEG_FILL)
                )
                t1 = dot_t(x_h, dy_h) * decay
                dg = dg + t1
                mt = t1 * gt
                from_state = dot(b_low, ds_low)
                dx = dot((gt * decay).astype(BF16), dy_h) + from_state * tail[:, h : h + 1]
                dx_ref[span, lanes_of(h)] = dx.astype(BF16)
                edy_h = (dy_h.astype(F32) * grow[:, h : h + 1]).astype(BF16)
                r2 = tail_x.astype(F32) * from_state
                column = jnp.sum(
                    edy_h.astype(F32) * dot(c_low, state) - r2 - mt, axis=1, keepdims=True
                )
                columns = jnp.where(column_at == h, column, columns)
                row_sums = jnp.where(row_at == h, jnp.sum(mt, axis=0, keepdims=True), row_sums)
                total = jnp.sum(r2, axis=0, keepdims=True) + whole[:, h : h + 1] * jnp.sum(
                    ds_wide * state.astype(F32), axis=0, keepdims=True
                )
                totals = jnp.where(row_at == h, total, totals)
                dc = dc + dot_t(edy_h, state)
                db = db + dot_t(tail_x, ds_low)
                ds_all[c, :, lanes] = ds_wide * whole[:, h : h + 1] + dot(c_t, edy_h)
            dgt[at] += dg
            db_ref[g, span, :] += db
            dc_ref[g, span, :] += dc
            total = jnp.sum(totals, axis=1, keepdims=True)
            row_sums = row_sums + jnp.where(
                iota2((all_heads, BLOCK), 1) == BLOCK - 1, total, 0.0
            )
            da_ref[span, :] += columns + row_sums.T
            return carry

        lax.fori_loop(0, count, backward, 0)

    def turn(t, carry):
        @pl.when(t < chunks)
        def _():
            swap(t).wait_recv()

        @pl.when(t + ahead < chunks)
        def _():
            swap(t + ahead).start()

        cf = t - pair

        @pl.when((cf >= 0) & (cf < chunks))
        def _():
            forward_link(cf)

        cb = t - (pairs - 1 - pair)

        @pl.when((cb >= 0) & (cb < chunks))
        def _():
            backward_link(cb)

        done = t - (pairs - 1)

        @pl.when(done >= 0)
        def _():
            scan_chunk(done)

        return carry

    lax.fori_loop(0, chunks + pairs - 1, turn, 0)

    def finish(at, carry):
        g = at // count
        span = pl.ds(pl.multiple_of((at - g * count) * BLOCK, BLOCK), BLOCK)
        dg = dgt[at]
        db_ref[g, span, :] += dot_hi(dg, c_ref[g, span, :])
        dc_ref[g, span, :] += dot_hi(dg.T, b_ref[g, span, :])
        return carry

    lax.fori_loop(0, groups * count, finish, 0)

    for k in range(count):
        span = pl.ds(k * BLOCK, BLOCK)
        da_ref[span, :] = dot_hi(upper, da_ref[span, :])

    def settle(c, carry):
        swap(c).wait_send()
        pl.when(has_up)(lambda: climb(c).wait_send())
        pl.when(has_down)(lambda: descend(c).wait_send())
        return carry

    lax.fori_loop(0, chunks, settle, 0)


def attention_kernel(
    place_ref, own_ref, q_ref, do_ref, kv_ref, dq_ref, dkv_ref, scores, probs, acc
):
    halves, lanes_q, width = q_ref.shape
    half = kv_ref.shape[0] // place_ref.shape[0]
    scale = width ** (-0.5)
    rate = scale * math.log2(math.e)
    acc[...] = jnp.zeros_like(acc)
    visible = iota2((half, lanes_q), 0) <= lax.rem(iota2((half, lanes_q), 1), half)

    def rows_of(j):
        return pl.ds(pl.multiple_of(place_ref[j] * half, half), half)

    def fold(op, tile):
        return op(tile.reshape(half // 8, 8, lanes_q), axis=0)

    for i in range(halves):
        own = own_ref[i]
        q = q_ref[i]
        q_t = q.T

        def score(j):
            return dot(kv_ref[rows_of(j), :width], q_t)

        def first(j, top):
            tile = score(j)
            scores[j] = tile
            return jnp.maximum(top, fold(jnp.max, tile))

        tile = jnp.where(visible, score(own), NEG_FILL)
        scores[own] = tile
        top = lax.fori_loop(0, own, first, fold(jnp.max, tile))
        top = jnp.max(top, axis=0, keepdims=True) * rate

        def second(j, carry):
            sums, out_t = carry
            prob = jnp.exp2(scores[j] * rate - top)
            low = prob.astype(BF16)
            probs[j] = low
            value_t = kv_ref[rows_of(j), width:].T
            return (sums + fold(jnp.sum, prob), out_t + dot(value_t, low))

        sums, out_t = lax.fori_loop(
            0,
            own + 1,
            second,
            (jnp.zeros((8, lanes_q), F32), jnp.zeros((width, lanes_q), F32)),
        )
        inverse = 1.0 / jnp.sum(sums, axis=0, keepdims=True)
        do_t = do_ref[i].astype(F32).T
        out_low = (out_t * inverse).astype(BF16).astype(F32)
        delta = jnp.sum(do_t * out_low, axis=0, keepdims=True) * inverse
        do_scaled = do_t * inverse
        do_t_low = do_scaled.astype(BF16)
        do_low = do_scaled.T.astype(BF16)

        def third(j, dq_t):
            at = rows_of(j)
            key = kv_ref[at, :width]
            prob = probs[j]
            prob_grad = dot(kv_ref[at, width:], do_t_low)
            ds = (prob.astype(F32) * (prob_grad - delta)).astype(BF16)
            acc[at, :width] += dot(ds, q)
            acc[at, width:] += dot(prob, do_low)
            return dq_t + dot(key.T, ds)

        dq_t = lax.fori_loop(0, own + 1, third, jnp.zeros((width, lanes_q), F32))
        dq_ref[i] = (dq_t * scale).T.astype(BF16)

    quarters, devices, rows = dkv_ref.shape[:3]
    for d in range(devices):
        for u in range(quarters):
            span = pl.ds((d * quarters + u) * rows, rows)
            dkv_ref[u, d, :, :width] = (acc[span, :width] * scale).astype(BF16)
            dkv_ref[u, d, :, width:] = acc[span, width:].astype(BF16)


def pair_decays(log_decay, chunks, width):
    count = lax.axis_size("seq")
    is_odd = lax.axis_index("seq") % 2 == 1
    own = jnp.sum(log_decay, axis=0, keepdims=True)
    other = lax.ppermute(own, "seq", [(i, i ^ 1) for i in range(count)])
    first = jnp.where(is_odd, other, own)
    second = jnp.where(is_odd, own, other)
    decays = jnp.repeat(jnp.exp(jnp.concatenate([first, second])), width, axis=1)
    return decays.reshape(2, chunks, -1).transpose(1, 0, 2)


def per_device(
    ssd_input,
    log_decay,
    input_map,
    output_map,
    ssd_cotangent,
    queries,
    key_rows,
    value_rows,
    attn_cotangent,
    pair_order,
):
    count = lax.axis_size("seq")
    place = lax.axis_index("seq")
    rows, heads, width = ssd_input.shape
    groups, size = input_map.shape[1:]
    per = heads // groups
    span = per * width
    q_rows, q_heads, q_width = queries.shape
    half = q_rows // 2

    quarters = lax.axis_size("head")
    share = q_rows // quarters
    kv = jnp.concatenate([key_rows, value_rows], axis=1)
    kv = lax.dynamic_slice_in_dim(kv, lax.axis_index("head") * share, share, 0)
    kv = lax.all_gather(lax.all_gather(kv, "seq"), "head", axis=1, tiled=True)
    kv = kv.reshape(count * q_rows, 2 * q_width)

    chunk = min(4, per)
    chunks = heads // chunk
    per_chunks = per // chunk
    step = chunk * width
    decays = pair_decays(log_decay, chunks, width)
    x = ssd_input.reshape(rows, heads * width)
    dy = ssd_cotangent.reshape(rows, heads * width)
    a = log_decay.reshape(rows, groups, per).transpose(1, 0, 2)
    a_t = log_decay.T
    b = input_map.transpose(1, 0, 2)
    c = output_map.transpose(1, 0, 2)

    wide_spec = pl.BlockSpec((rows, span), lambda g: (0, g))
    a_spec = pl.BlockSpec((1, rows, per), lambda g: (g, 0, 0))
    map_spec = pl.BlockSpec((1, rows, size), lambda g: (g, 0, 0))
    state_flops = 4 * rows * heads * width * size
    sp = pl.pallas_call(
        state_kernel,
        grid=(groups,),
        in_specs=[wide_spec, wide_spec, a_spec, map_spec, map_spec],
        out_specs=pl.BlockSpec((per_chunks, 2, size, step), lambda g: (g, 0, 0, 0)),
        out_shape=jax.ShapeDtypeStruct((chunks, 2, size, step), BF16),
        scratch_shapes=[pltpu.VMEM((rows, span), BF16), pltpu.VMEM((rows, span), BF16)],
        compiler_params=pltpu.CompilerParams(vmem_limit_bytes=VMEM_BYTES),
        cost_estimate=pl.CostEstimate(
            flops=state_flops, bytes_accessed=4 * rows * heads * width, transcendentals=0
        ),
    )(x, dy, a, b, c)

    blocks = 2 * count
    own_first = pair_order[place]
    own = jnp.stack([own_first, blocks - 1 - own_first]).astype(jnp.int32)
    ids = jnp.stack([pair_order, blocks - 1 - pair_order], axis=1).reshape(-1)
    block_ids = jnp.arange(blocks, dtype=jnp.int32)
    where_at = jnp.sum(
        jnp.where(ids[None, :] == block_ids[:, None], block_ids[None, :], 0), axis=1
    ).astype(jnp.int32)

    def by_half(array):
        parts = array.reshape(2, half, q_heads, q_width).transpose(0, 2, 1, 3)
        return parts.reshape(2, q_heads * half, q_width)

    vmem = pl.BlockSpec(memory_space=pltpu.VMEM)
    smem = pl.BlockSpec(memory_space=pltpu.SMEM)
    lanes_q = q_heads * half
    dq, dkv = pl.pallas_call(
        attention_kernel,
        in_specs=[smem, smem, vmem, vmem, vmem],
        out_specs=[vmem, vmem],
        out_shape=[
            jax.ShapeDtypeStruct((2, lanes_q, q_width), BF16),
            jax.ShapeDtypeStruct((quarters, count, q_rows // quarters, 2 * q_width), BF16),
        ],
        scratch_shapes=[
            pltpu.VMEM((blocks, half, lanes_q), F32),
            pltpu.VMEM((blocks, half, lanes_q), BF16),
            pltpu.VMEM((count * q_rows, 2 * q_width), F32),
        ],
        compiler_params=pltpu.CompilerParams(vmem_limit_bytes=VMEM_BYTES),
        cost_estimate=pl.CostEstimate(
            flops=12 * (blocks + 1) * half * lanes_q * q_width,
            bytes_accessed=4 * count * q_rows * q_width * 4,
            transcendentals=(blocks + 1) * half * lanes_q,
        ),
    )(where_at, own, by_half(queries), by_half(attn_cotangent), kv)

    sp, dkv = lax.optimization_barrier((sp, dkv))
    dkv = dkv.reshape(quarters * count * share, 2 * q_width)
    dkv = lax.psum_scatter(dkv, ("head", "seq"), scatter_dimension=0, tiled=True)
    dkv = lax.all_gather(dkv, "head", axis=0, tiled=True)
    grad_keys = dkv[:, :q_width]
    grad_values = dkv[:, q_width:]
    grad_queries = (
        dq.reshape(2, q_heads, half, q_width).transpose(0, 2, 1, 3).reshape(queries.shape)
    )

    pairs = count // 2
    parts = rows // BLOCK
    sems = [pltpu.SemaphoreType.DMA((chunks,)) for _ in range(6)]
    dx, da, db, dc = pl.pallas_call(
        functools.partial(scan_kernel, pairs),
        in_specs=[vmem] * 8,
        out_specs=[vmem] * 4,
        out_shape=[
            jax.ShapeDtypeStruct((rows, heads * width), BF16),
            jax.ShapeDtypeStruct((rows, heads), F32),
            jax.ShapeDtypeStruct((groups, rows, size), F32),
            jax.ShapeDtypeStruct((groups, rows, size), F32),
        ],
        scratch_shapes=[
            pltpu.VMEM((chunks, 2, size, step), BF16),
            pltpu.VMEM((chunks, size, step), BF16),
            pltpu.VMEM((chunks, size, step), BF16),
            pltpu.VMEM((chunks, size, step), BF16),
            pltpu.VMEM((chunks, size, step), BF16),
            pltpu.VMEM((parts, size, step), BF16),
            pltpu.VMEM((rows, step), BF16),
            pltpu.VMEM((chunks, size, step), F32),
            pltpu.VMEM((chunks, size, step), F32),
            pltpu.VMEM((groups * parts, BLOCK, BLOCK), F32),
            pltpu.VMEM((groups * parts, BLOCK, BLOCK), F32),
            pltpu.VMEM((groups * parts, 2, BLOCK, size), BF16),
            pltpu.VMEM((groups * parts, 2, size, BLOCK), BF16),
            pltpu.VMEM((chunks, rows, chunk), F32),
            pltpu.VMEM((chunks, chunk, rows), F32),
            *sems,
        ],
        compiler_params=pltpu.CompilerParams(
            vmem_limit_bytes=VMEM_BYTES, collective_id=0, has_side_effects=True
        ),
        cost_estimate=pl.CostEstimate(
            flops=5 * state_flops,
            bytes_accessed=8 * rows * heads * width,
            transcendentals=rows * heads * BLOCK,
        ),
    )(x, dy, log_decay, a_t, b, c, sp, decays)

    return (
        dx.reshape(rows, heads, width),
        da,
        db.transpose(1, 0, 2),
        dc.transpose(1, 0, 2),
        grad_queries,
        grad_keys,
        grad_values,
    )


def solution(mesh):
    return jax.shard_map(
        per_device,
        mesh=mesh,
        in_specs=(
            P("seq", "head", None),
            P("seq", "head"),
            P("seq", "head", None),
            P("seq", "head", None),
            P("seq", "head", None),
            P("seq", "head", None),
            P("seq", None),
            P("seq", None),
            P("seq", "head", None),
            P(),
        ),
        out_specs=(
            P("seq", "head", None),
            P("seq", "head"),
            P("seq", "head", None),
            P("seq", "head", None),
            P("seq", "head", None),
            P("seq", None),
            P("seq", None),
        ),
        check_vma=False,
    )
```

```python
import functools
import math

import jax
import jax.numpy as jnp
from jax import lax
from jax.experimental import pallas as pl
from jax.experimental.pallas import tpu as pltpu
from jax.sharding import PartitionSpec as P

BLOCK = 128
HIGHEST = lax.Precision.HIGHEST
NEG_FILL = -1e30
F32 = jnp.float32
BF16 = jnp.bfloat16
VMEM_BYTES = 52 * 1024 * 1024


def dot(a, b):
    return jnp.dot(a, b, preferred_element_type=F32)


def dot_t(a, b):
    return lax.dot_general(a, b, (((1,), (1,)), ((), ())), preferred_element_type=F32)


def dot_hi(a, b):
    return jnp.dot(a, b, preferred_element_type=F32, precision=HIGHEST)


def iota2(shape, dim):
    return lax.broadcasted_iota(jnp.int32, shape, dim)


def lower_ones():
    shape = (BLOCK, BLOCK)
    return (iota2(shape, 0) >= iota2(shape, 1)).astype(F32)


def upper_ones():
    shape = (BLOCK, BLOCK)
    return (iota2(shape, 0) <= iota2(shape, 1)).astype(F32)


def state_kernel(x_ref, dy_ref, a_ref, b_ref, c_ref, sp_ref, tx, ey):
    rows, heads = a_ref.shape[1:]
    width = x_ref.shape[1] // heads
    lower = lower_ones()
    offset = jnp.zeros((1, heads), F32)
    cums = []
    for k in range(rows // BLOCK):
        cum = dot_hi(lower, a_ref[0, pl.ds(k * BLOCK, BLOCK), :])
        cums.append(cum + offset)
        offset = offset + cum[BLOCK - 1 :, :]
    for k, cum in enumerate(cums):
        span = pl.ds(k * BLOCK, BLOCK)
        tail = jnp.exp(offset - cum)
        head_decay = jnp.exp(cum)
        for h in range(heads):
            lanes = pl.ds(h * width, width)
            tx[span, lanes] = (x_ref[span, lanes].astype(F32) * tail[:, h : h + 1]).astype(BF16)
            ey[span, lanes] = (
                dy_ref[span, lanes].astype(F32) * head_decay[:, h : h + 1]
            ).astype(BF16)
    b_t = b_ref[0].T.astype(BF16)
    c_t = c_ref[0].T.astype(BF16)
    chunks, _, _, step = sp_ref.shape
    for at in range(chunks):
        lanes = pl.ds(at * step, step)
        sp_ref[at, 0] = dot(b_t, tx[:, lanes]).astype(BF16)
        sp_ref[at, 1] = dot(c_t, ey[:, lanes]).astype(BF16)


def scan_kernel(
    pairs,
    x_ref,
    dy_ref,
    a_ref,
    at_ref,
    b_ref,
    c_ref,
    sp_ref,
    w_ref,
    dx_ref,
    da_ref,
    db_ref,
    dc_ref,
    y_in,
    f_in,
    b_in,
    f_out,
    b_out,
    states,
    tails,
    s_all,
    ds_all,
    gts,
    dgt,
    maps_low,
    maps_t,
    cums,
    cums_t,
    y_send,
    y_recv,
    f_send,
    f_recv,
    b_send,
    b_recv,
):
    chunks = sp_ref.shape[0]
    rows, all_heads = a_ref.shape
    heads = all_heads // chunks
    groups, _, size = b_ref.shape
    per_group = chunks // groups
    width = x_ref.shape[1] // (chunks * heads)
    count = rows // BLOCK
    me = lax.axis_index("seq")
    pair = me // 2
    odd = me - 2 * pair
    partner = me + 1 - 2 * odd
    up = me + 2
    down = me - 2
    has_up = pair < pairs - 1
    has_down = pair > 0

    barrier = pltpu.get_barrier_semaphore()

    def greet(device):
        pl.semaphore_signal(
            barrier, inc=1, device_id={"seq": device}, device_id_type=pl.DeviceIdType.MESH
        )

    greet(partner)
    pl.when(has_up)(lambda: greet(up))
    pl.when(has_down)(lambda: greet(down))
    pl.semaphore_wait(barrier, 1 + has_up.astype(jnp.int32) + has_down.astype(jnp.int32))

    def remote(src, dst, send, recv, c, device):
        return pltpu.make_async_remote_copy(
            src_ref=src.at[c],
            dst_ref=dst.at[c],
            send_sem=send.at[c],
            recv_sem=recv.at[c],
            device_id={"seq": device},
            device_id_type=pl.DeviceIdType.MESH,
        )

    def swap(c):
        return remote(sp_ref, y_in, y_send, y_recv, c, partner)

    def climb(c):
        return remote(f_out, f_in, f_send, f_recv, c, up)

    def descend(c):
        return remote(b_out, b_in, b_send, b_recv, c, down)

    ahead = min(2, chunks)
    for c in range(ahead):
        swap(c).start()

    lower = lower_ones()
    upper = upper_ones()
    causal = iota2((BLOCK, BLOCK), 0) <= iota2((BLOCK, BLOCK), 1)
    db_ref[...] = jnp.zeros_like(db_ref)
    dc_ref[...] = jnp.zeros_like(dc_ref)
    dgt[...] = jnp.zeros_like(dgt)
    da_ref[...] = jnp.zeros_like(da_ref)
    for k in range(count):
        span = pl.ds(k * BLOCK, BLOCK)
        cum = dot_hi(lower, a_ref[span, :])
        cum_t = dot_hi(at_ref[:, span], upper)
        for c in range(chunks):
            cums[c, span, :] = cum[:, c * heads : (c + 1) * heads]
            cums_t[c, :, span] = cum_t[c * heads : (c + 1) * heads, :]

    def prepare(at, carry):
        g = at // count
        span = pl.ds(pl.multiple_of((at - g * count) * BLOCK, BLOCK), BLOCK)
        b_wide = b_ref[g, span, :]
        c_wide = c_ref[g, span, :]
        gts[at] = lax.dot_general(
            b_wide, c_wide, (((1,), (1,)), ((), ())), preferred_element_type=F32, precision=HIGHEST
        )
        maps_low[at, 0] = b_wide.astype(BF16)
        maps_low[at, 1] = c_wide.astype(BF16)
        maps_t[at, 0] = b_wide.T.astype(BF16)
        maps_t[at, 1] = c_wide.T.astype(BF16)
        return carry

    lax.fori_loop(0, groups * count, prepare, 0)
    is_odd = odd == 1

    def forward_link(c):
        own = sp_ref[c, 0].astype(F32)
        other = y_in[c, 0].astype(F32)
        first = jnp.where(is_odd, other, own)
        second = jnp.where(is_odd, own, other)
        w_first = w_ref[c, 0:1, :]
        w_second = w_ref[c, 1:2, :]
        f_out[c] = (first * w_second + second).astype(BF16)
        s_all[c] = jnp.where(is_odd, first, 0.0)

        @pl.when(has_down)
        def _():
            climb(c).wait_recv()
            arrived = f_in[c].astype(F32)
            s_all[c] = jnp.where(is_odd, arrived * w_first + first, arrived)
            total = first * w_second + second + arrived * (w_first * w_second)
            f_out[c] = total.astype(BF16)

        pl.when(has_up)(lambda: climb(c).start())

    def backward_link(c):
        own = sp_ref[c, 1].astype(F32)
        other = y_in[c, 1].astype(F32)
        first = jnp.where(is_odd, other, own)
        second = jnp.where(is_odd, own, other)
        w_first = w_ref[c, 0:1, :]
        w_second = w_ref[c, 1:2, :]
        b_out[c] = (first + second * w_first).astype(BF16)
        ds_all[c] = jnp.where(is_odd, 0.0, second)

        @pl.when(has_up)
        def _():
            descend(c).wait_recv()
            arrived = b_in[c].astype(F32)
            ds_all[c] = jnp.where(is_odd, arrived, arrived * w_second + second)
            total = first + second * w_first + arrived * (w_first * w_second)
            b_out[c] = total.astype(BF16)

        pl.when(has_down)(lambda: descend(c).start())

    def scan_chunk(c):
        g = c // per_group
        base = c * (heads * width)

        def lanes_of(h):
            return pl.ds(pl.multiple_of(base + h * width, width), width)

        def forward(k, carry):
            span = pl.ds(pl.multiple_of(k * BLOCK, BLOCK), BLOCK)
            cum = cums[c, span, :]
            last = cum[BLOCK - 1 :, :]
            tail = jnp.exp(last - cum)
            whole = jnp.exp(last)
            b_t = maps_t[g * count + k, 0]
            for h in range(heads):
                lanes = pl.ds(h * width, width)
                tail_x = (x_ref[span, lanes_of(h)].astype(F32) * tail[:, h : h + 1]).astype(BF16)
                tails[span, lanes] = tail_x
                now = s_all[c, :, lanes]
                states[k, :, lanes] = now.astype(BF16)
                s_all[c, :, lanes] = now * whole[:, h : h + 1] + dot(b_t, tail_x)
            return carry

        lax.fori_loop(0, count, forward, 0)

        def backward(turn, carry):
            k = count - 1 - turn
            at = g * count + k
            span = pl.ds(pl.multiple_of(k * BLOCK, BLOCK), BLOCK)
            cum = cums[c, span, :]
            cum_t = cums_t[c, :, span]
            last = cum[BLOCK - 1 :, :]
            tail = jnp.exp(last - cum)
            whole = jnp.exp(last)
            grow = jnp.exp(cum)
            b_low = maps_low[at, 0]
            c_low = maps_low[at, 1]
            c_t = maps_t[at, 1]
            gt = gts[at]
            columns = jnp.zeros((BLOCK, all_heads), F32)
            row_sums = jnp.zeros((all_heads, BLOCK), F32)
            totals = jnp.zeros((all_heads, BLOCK), F32)
            column_at = iota2((BLOCK, all_heads), 1) - c * heads
            row_at = iota2((all_heads, BLOCK), 0) - c * heads
            db = jnp.zeros((BLOCK, size), F32)
            dc = jnp.zeros((BLOCK, size), F32)
            dg = jnp.zeros((BLOCK, BLOCK), F32)
            for h in range(heads):
                lanes = pl.ds(h * width, width)
                x_h = x_ref[span, lanes_of(h)]
                dy_h = dy_ref[span, lanes_of(h)]
                tail_x = tails[span, lanes]
                state = states[k, :, lanes]
                ds_wide = ds_all[c, :, lanes]
                ds_low = ds_wide.astype(BF16)
                decay = jnp.exp(
                    jnp.where(causal, cum_t[h : h + 1, :] - cum[:, h : h + 1], NEG_FILL)
                )
                t1 = dot_t(x_h, dy_h) * decay
                dg = dg + t1
                mt = t1 * gt
                from_state = dot(b_low, ds_low)
                dx = dot((gt * decay).astype(BF16), dy_h) + from_state * tail[:, h : h + 1]
                dx_ref[span, lanes_of(h)] = dx.astype(BF16)
                edy_h = (dy_h.astype(F32) * grow[:, h : h + 1]).astype(BF16)
                r2 = tail_x.astype(F32) * from_state
                column = jnp.sum(
                    edy_h.astype(F32) * dot(c_low, state) - r2 - mt, axis=1, keepdims=True
                )
                columns = jnp.where(column_at == h, column, columns)
                row_sums = jnp.where(row_at == h, jnp.sum(mt, axis=0, keepdims=True), row_sums)
                total = jnp.sum(r2, axis=0, keepdims=True) + whole[:, h : h + 1] * jnp.sum(
                    ds_wide * state.astype(F32), axis=0, keepdims=True
                )
                totals = jnp.where(row_at == h, total, totals)
                dc = dc + dot_t(edy_h, state)
                db = db + dot_t(tail_x, ds_low)
                ds_all[c, :, lanes] = ds_wide * whole[:, h : h + 1] + dot(c_t, edy_h)
            dgt[at] += dg
            db_ref[g, span, :] += db
            dc_ref[g, span, :] += dc
            total = jnp.sum(totals, axis=1, keepdims=True)
            row_sums = row_sums + jnp.where(
                iota2((all_heads, BLOCK), 1) == BLOCK - 1, total, 0.0
            )
            da_ref[span, :] += columns + row_sums.T
            return carry

        lax.fori_loop(0, count, backward, 0)

    def turn(t, carry):
        @pl.when(t < chunks)
        def _():
            swap(t).wait_recv()

        @pl.when(t + ahead < chunks)
        def _():
            swap(t + ahead).start()

        cf = t - pair

        @pl.when((cf >= 0) & (cf < chunks))
        def _():
            forward_link(cf)

        cb = t - (pairs - 1 - pair)

        @pl.when((cb >= 0) & (cb < chunks))
        def _():
            backward_link(cb)

        done = t - (pairs - 1)

        @pl.when(done >= 0)
        def _():
            scan_chunk(done)

        return carry

    lax.fori_loop(0, chunks + pairs - 1, turn, 0)

    def finish(at, carry):
        g = at // count
        span = pl.ds(pl.multiple_of((at - g * count) * BLOCK, BLOCK), BLOCK)
        dg = dgt[at]
        db_ref[g, span, :] += dot_hi(dg, c_ref[g, span, :])
        dc_ref[g, span, :] += dot_hi(dg.T, b_ref[g, span, :])
        return carry

    lax.fori_loop(0, groups * count, finish, 0)

    for k in range(count):
        span = pl.ds(k * BLOCK, BLOCK)
        da_ref[span, :] = dot_hi(upper, da_ref[span, :])

    def settle(c, carry):
        swap(c).wait_send()
        pl.when(has_up)(lambda: climb(c).wait_send())
        pl.when(has_down)(lambda: descend(c).wait_send())
        return carry

    lax.fori_loop(0, chunks, settle, 0)


def attention_kernel(
    place_ref, own_ref, q_ref, do_ref, kv_ref, dq_ref, dkv_ref, scores, probs, acc
):
    halves, lanes_q, width = q_ref.shape
    half = kv_ref.shape[0] // place_ref.shape[0]
    scale = width ** (-0.5)
    rate = scale * math.log2(math.e)
    acc[...] = jnp.zeros_like(acc)
    visible = iota2((half, lanes_q), 0) <= lax.rem(iota2((half, lanes_q), 1), half)

    def rows_of(j):
        return pl.ds(pl.multiple_of(place_ref[j] * half, half), half)

    def fold(op, tile):
        return op(tile.reshape(half // 8, 8, lanes_q), axis=0)

    for i in range(halves):
        own = own_ref[i]
        q = q_ref[i]
        q_t = q.T

        def score(j):
            return dot(kv_ref[rows_of(j), :width], q_t)

        def first(j, top):
            tile = score(j)
            scores[j] = tile
            return jnp.maximum(top, fold(jnp.max, tile))

        tile = jnp.where(visible, score(own), NEG_FILL)
        scores[own] = tile
        top = lax.fori_loop(0, own, first, fold(jnp.max, tile))
        top = jnp.max(top, axis=0, keepdims=True) * rate

        def second(j, carry):
            sums, out_t = carry
            prob = jnp.exp2(scores[j] * rate - top)
            low = prob.astype(BF16)
            probs[j] = low
            value_t = kv_ref[rows_of(j), width:].T
            return (sums + fold(jnp.sum, prob), out_t + dot(value_t, low))

        sums, out_t = lax.fori_loop(
            0,
            own + 1,
            second,
            (jnp.zeros((8, lanes_q), F32), jnp.zeros((width, lanes_q), F32)),
        )
        inverse = 1.0 / jnp.sum(sums, axis=0, keepdims=True)
        do_t = do_ref[i].astype(F32).T
        out_low = (out_t * inverse).astype(BF16).astype(F32)
        delta = jnp.sum(do_t * out_low, axis=0, keepdims=True) * inverse
        do_scaled = do_t * inverse
        do_t_low = do_scaled.astype(BF16)
        do_low = do_scaled.T.astype(BF16)

        def third(j, dq_t):
            at = rows_of(j)
            key = kv_ref[at, :width]
            prob = probs[j]
            prob_grad = dot(kv_ref[at, width:], do_t_low)
            ds = (prob.astype(F32) * (prob_grad - delta)).astype(BF16)
            acc[at, :width] += dot(ds, q)
            acc[at, width:] += dot(prob, do_low)
            return dq_t + dot(key.T, ds)

        dq_t = lax.fori_loop(0, own + 1, third, jnp.zeros((width, lanes_q), F32))
        dq_ref[i] = (dq_t * scale).T.astype(BF16)

    quarters, devices, rows = dkv_ref.shape[:3]
    for d in range(devices):
        for u in range(quarters):
            span = pl.ds((d * quarters + u) * rows, rows)
            dkv_ref[u, d, :, :width] = (acc[span, :width] * scale).astype(BF16)
            dkv_ref[u, d, :, width:] = acc[span, width:].astype(BF16)


def pair_decays(log_decay, chunks, width):
    count = lax.axis_size("seq")
    is_odd = lax.axis_index("seq") % 2 == 1
    own = jnp.sum(log_decay, axis=0, keepdims=True)
    other = lax.ppermute(own, "seq", [(i, i ^ 1) for i in range(count)])
    first = jnp.where(is_odd, other, own)
    second = jnp.where(is_odd, own, other)
    decays = jnp.repeat(jnp.exp(jnp.concatenate([first, second])), width, axis=1)
    return decays.reshape(2, chunks, -1).transpose(1, 0, 2)


def per_device(
    ssd_input,
    log_decay,
    input_map,
    output_map,
    ssd_cotangent,
    queries,
    key_rows,
    value_rows,
    attn_cotangent,
    pair_order,
):
    count = lax.axis_size("seq")
    place = lax.axis_index("seq")
    rows, heads, width = ssd_input.shape
    groups, size = input_map.shape[1:]
    per = heads // groups
    span = per * width
    q_rows, q_heads, q_width = queries.shape
    half = q_rows // 2

    quarters = lax.axis_size("head")
    kv = lax.all_gather(
        jnp.concatenate([key_rows, value_rows], axis=1), "seq", axis=0, tiled=True
    )

    chunk = min(4, per)
    chunks = heads // chunk
    per_chunks = per // chunk
    step = chunk * width
    decays = pair_decays(log_decay, chunks, width)
    x = ssd_input.reshape(rows, heads * width)
    dy = ssd_cotangent.reshape(rows, heads * width)
    a = log_decay.reshape(rows, groups, per).transpose(1, 0, 2)
    a_t = log_decay.T
    b = input_map.transpose(1, 0, 2)
    c = output_map.transpose(1, 0, 2)

    wide_spec = pl.BlockSpec((rows, span), lambda g: (0, g))
    a_spec = pl.BlockSpec((1, rows, per), lambda g: (g, 0, 0))
    map_spec = pl.BlockSpec((1, rows, size), lambda g: (g, 0, 0))
    state_flops = 4 * rows * heads * width * size
    sp = pl.pallas_call(
        state_kernel,
        grid=(groups,),
        in_specs=[wide_spec, wide_spec, a_spec, map_spec, map_spec],
        out_specs=pl.BlockSpec((per_chunks, 2, size, step), lambda g: (g, 0, 0, 0)),
        out_shape=jax.ShapeDtypeStruct((chunks, 2, size, step), BF16),
        scratch_shapes=[pltpu.VMEM((rows, span), BF16), pltpu.VMEM((rows, span), BF16)],
        compiler_params=pltpu.CompilerParams(vmem_limit_bytes=VMEM_BYTES),
        cost_estimate=pl.CostEstimate(
            flops=state_flops, bytes_accessed=4 * rows * heads * width, transcendentals=0
        ),
    )(x, dy, a, b, c)

    blocks = 2 * count
    own_first = pair_order[place]
    own = jnp.stack([own_first, blocks - 1 - own_first]).astype(jnp.int32)
    ids = jnp.stack([pair_order, blocks - 1 - pair_order], axis=1).reshape(-1)
    block_ids = jnp.arange(blocks, dtype=jnp.int32)
    where_at = jnp.sum(
        jnp.where(ids[None, :] == block_ids[:, None], block_ids[None, :], 0), axis=1
    ).astype(jnp.int32)

    def by_half(array):
        parts = array.reshape(2, half, q_heads, q_width).transpose(0, 2, 1, 3)
        return parts.reshape(2, q_heads * half, q_width)

    vmem = pl.BlockSpec(memory_space=pltpu.VMEM)
    smem = pl.BlockSpec(memory_space=pltpu.SMEM)
    lanes_q = q_heads * half
    dq, dkv = pl.pallas_call(
        attention_kernel,
        in_specs=[smem, smem, vmem, vmem, vmem],
        out_specs=[vmem, vmem],
        out_shape=[
            jax.ShapeDtypeStruct((2, lanes_q, q_width), BF16),
            jax.ShapeDtypeStruct((quarters, count, q_rows // quarters, 2 * q_width), BF16),
        ],
        scratch_shapes=[
            pltpu.VMEM((blocks, half, lanes_q), F32),
            pltpu.VMEM((blocks, half, lanes_q), BF16),
            pltpu.VMEM((count * q_rows, 2 * q_width), F32),
        ],
        compiler_params=pltpu.CompilerParams(vmem_limit_bytes=VMEM_BYTES),
        cost_estimate=pl.CostEstimate(
            flops=12 * (blocks + 1) * half * lanes_q * q_width,
            bytes_accessed=4 * count * q_rows * q_width * 4,
            transcendentals=(blocks + 1) * half * lanes_q,
        ),
    )(where_at, own, by_half(queries), by_half(attn_cotangent), kv)

    sp, dkv = lax.optimization_barrier((sp, dkv))
    dkv = lax.psum_scatter(dkv, "head", scatter_dimension=0, tiled=True)[0]
    dkv = lax.psum_scatter(dkv, "seq", scatter_dimension=0, tiled=True)[0]
    dkv = lax.all_gather(dkv, "head", axis=0, tiled=True)
    grad_keys = dkv[:, :q_width]
    grad_values = dkv[:, q_width:]
    grad_queries = (
        dq.reshape(2, q_heads, half, q_width).transpose(0, 2, 1, 3).reshape(queries.shape)
    )

    pairs = count // 2
    parts = rows // BLOCK
    sems = [pltpu.SemaphoreType.DMA((chunks,)) for _ in range(6)]
    dx, da, db, dc = pl.pallas_call(
        functools.partial(scan_kernel, pairs),
        in_specs=[vmem] * 8,
        out_specs=[vmem] * 4,
        out_shape=[
            jax.ShapeDtypeStruct((rows, heads * width), BF16),
            jax.ShapeDtypeStruct((rows, heads), F32),
            jax.ShapeDtypeStruct((groups, rows, size), F32),
            jax.ShapeDtypeStruct((groups, rows, size), F32),
        ],
        scratch_shapes=[
            pltpu.VMEM((chunks, 2, size, step), BF16),
            pltpu.VMEM((chunks, size, step), BF16),
            pltpu.VMEM((chunks, size, step), BF16),
            pltpu.VMEM((chunks, size, step), BF16),
            pltpu.VMEM((chunks, size, step), BF16),
            pltpu.VMEM((parts, size, step), BF16),
            pltpu.VMEM((rows, step), BF16),
            pltpu.VMEM((chunks, size, step), F32),
            pltpu.VMEM((chunks, size, step), F32),
            pltpu.VMEM((groups * parts, BLOCK, BLOCK), F32),
            pltpu.VMEM((groups * parts, BLOCK, BLOCK), F32),
            pltpu.VMEM((groups * parts, 2, BLOCK, size), BF16),
            pltpu.VMEM((groups * parts, 2, size, BLOCK), BF16),
            pltpu.VMEM((chunks, rows, chunk), F32),
            pltpu.VMEM((chunks, chunk, rows), F32),
            *sems,
        ],
        compiler_params=pltpu.CompilerParams(
            vmem_limit_bytes=VMEM_BYTES, collective_id=0, has_side_effects=True
        ),
        cost_estimate=pl.CostEstimate(
            flops=5 * state_flops,
            bytes_accessed=8 * rows * heads * width,
            transcendentals=rows * heads * BLOCK,
        ),
    )(x, dy, log_decay, a_t, b, c, sp, decays)

    return (
        dx.reshape(rows, heads, width),
        da,
        db.transpose(1, 0, 2),
        dc.transpose(1, 0, 2),
        grad_queries,
        grad_keys,
        grad_values,
    )


def solution(mesh):
    return jax.shard_map(
        per_device,
        mesh=mesh,
        in_specs=(
            P("seq", "head", None),
            P("seq", "head"),
            P("seq", "head", None),
            P("seq", "head", None),
            P("seq", "head", None),
            P("seq", "head", None),
            P("seq", None),
            P("seq", None),
            P("seq", "head", None),
            P(),
        ),
        out_specs=(
            P("seq", "head", None),
            P("seq", "head"),
            P("seq", "head", None),
            P("seq", "head", None),
            P("seq", "head", None),
            P("seq", None),
            P("seq", None),
        ),
        check_vma=False,
    )
```
